768 devices in a mesh: row: 192 (over y, z, core), col: 4 (over x).
Axes of the slice: x: 4, y: 8, z: 12, core: 2. Of those that a mesh axis runs over, the one named last changes fastest.
Arguments:
- tiles: bfloat16 [192, 4, 64, 128, 128], P('row', 'col'), may hold values from -0.3125 to 0.3125
- tile_model: int32 [192, 4, 64], P('row', 'col'), may hold values from 0 to 1535
- ray_counts: int32 [192, 4, 16], P('row', 'col'), may hold values from 1 to 4, as said below
- data: float32 [393216], P('row'), may hold values from -40 to 40
Outputs:
- model: float32 [4, 196608], P('col', 'row')
- ray_basis: float32 [393216], P('row')
The draws below stay inside these ranges and needn't reach their ends.
Inputs may be any that keep to these rules, and one draw needn't show every extreme that they name: `ray_counts`: each device's counts sum to at most 64; on some device every count is 4.
All inputs are finite; a program needn't handle non-finite values.
Results may differ from the reference program's by a relative error of at most 0.0051.
Values may be sent and summed in bfloat16 or wider, within the bound.
A program may use at most 32 MiB of HBM per device.

```python
import jax
import jax.numpy as jnp
from jax import lax

TILE = 128
TILES_DEV = 64
RB_DEV = 16
MB_DEV = 8
ITERS = 1
MB_COL = 1536
RAYS = 393216
N_ROW = 192
N_COL = 4


def draw_ray_counts(key, part):
    key = jax.random.fold_in(key, 11)
    k_level, k_count, k_row, k_col = jax.random.split(key, 4)
    ceiling = TILES_DEV // RB_DEV
    level = jax.random.randint(k_level, (N_ROW, N_COL, 1), 1, 5)
    upper = jnp.maximum(1, ceiling * level // 4)
    counts = jax.random.randint(k_count, (N_ROW, N_COL, RB_DEV), 1, upper + 1)
    full_row = jax.random.randint(k_row, (), 0, N_ROW)
    full_col = jax.random.randint(k_col, (), 0, N_COL)
    chosen = (jnp.arange(N_ROW)[:, None] == full_row) & (jnp.arange(N_COL)[None, :] == full_col)
    counts = jnp.where(chosen[:, :, None], ceiling, counts)
    return counts.astype(jnp.int32)


def draw_data(key, part):
    key = jax.random.fold_in(key, 23)
    k_value, k_scale = jax.random.split(key, 2)
    scales = jnp.exp(jax.random.uniform(k_scale, (RAYS,), jnp.float32, 0.0, 2.302585))
    out = jnp.clip(jax.random.normal(k_value, (RAYS,), jnp.float32), -4.0, 4.0) * scales
    return jnp.clip(out, -40.0, 40.0).astype(jnp.float32)


def set_ends(result, key, low, high):
    longest = result.shape.index(max(result.shape))
    spots = []
    for shift in (0, 1):
        where = [jax.random.randint(jax.random.fold_in(key, axis), (), 0, length) for axis, length in enumerate(result.shape)]
        where[longest] = (where[longest] + shift) % result.shape[longest]
        spots.append(tuple(where))
    return result.at[spots[0]].set(low).at[spots[1]].set(high)


def block_levels(rng, extent, cuts, low, high):
    factor_of, own = 1.0, jax.random.fold_in(rng, 6)
    for position, parts in cuts:
        steps = jnp.exp(jax.random.uniform(jax.random.fold_in(own, position), (parts,), jnp.float32, low / len(cuts), high / len(cuts)))
        factor_of = factor_of * jnp.repeat(steps, extent[position] // parts).reshape([-1 if axis == position else 1 for axis in range(len(extent))])
    return factor_of


def scatter_about(key, dims, deviation, reach, cuts=(), held_as=jnp.bfloat16):
    result = jax.random.normal(key, dims, jnp.float32) * deviation
    if len(cuts) > 0:
        result = block_levels(key, dims, cuts, -0.22, 0.18) * result
    return jnp.clip(result, min=-reach, max=reach).astype(held_as)


def setup_inputs(seed: int = 0) -> dict:
    keys = jax.random.split(jax.random.key(seed), 5)
    return {
        "tiles": scatter_about(keys[0], (N_ROW, N_COL, TILES_DEV, TILE, TILE), (TILE * TILES_DEV * 3 // (8 * MB_DEV)) ** -0.5, 0.3125, ((0, 192), (1, 4))),
        "tile_model": set_ends(jax.random.randint(keys[1], (N_ROW, N_COL, TILES_DEV), 0, MB_COL), jax.random.fold_in(keys[1], 1), 0, MB_COL - 1).astype(jnp.int32),
        "ray_counts": draw_ray_counts(jax.random.fold_in(keys[4], 71), 0),
        "data": draw_data(jax.random.fold_in(keys[4], 71), 0),
    }


EPS = 1e-06
HIGH = lax.Precision.HIGHEST

def slot_layout(counts):
    cum = jnp.cumsum(counts)
    slots = jnp.arange(TILES_DEV, dtype=jnp.int32)
    slot_ray = lax.optimization_barrier(jnp.sum((cum[None, :] <= slots[:, None]).astype(jnp.int32), axis=1))
    slot_ray = jnp.minimum(slot_ray, RB_DEV - 1).astype(jnp.int32)
    return (slot_ray, slots < cum[-1])

def forward(tiles, tile_model, ray_counts, column_half):

    def one_dev(panels, models, counts, vcol):
        slot_ray, valid = slot_layout(counts)
        table = ((slot_ray[None, :] == jnp.arange(RB_DEV, dtype=jnp.int32)[:, None]) & valid[None, :]).astype(jnp.float32)
        picked = vcol[models].astype(jnp.float32)
        prod = jnp.einsum('tij,tj->ti', panels.astype(jnp.float32), picked, precision=HIGH)
        return jnp.dot(table, prod, precision=HIGH)

    def one_row(items):
        panels, models, counts = items
        return lax.optimization_barrier(jnp.sum(jax.vmap(one_dev)(panels, models, counts, column_half), axis=0))
    return lax.map(one_row, (tiles, tile_model, ray_counts)).reshape(-1)

def backward(tiles, tile_model, ray_counts, ray_half):

    def step(carry, items):
        panels_r, models_r, counts_r, u_row = items

        def one_col(panels, models, counts):
            slot_ray, valid = slot_layout(counts)
            picked = u_row[slot_ray].astype(jnp.float32)
            prod = jnp.einsum('tij,ti->tj', panels.astype(jnp.float32), picked, precision=HIGH)
            prod = prod * valid.astype(jnp.float32)[:, None]
            return jax.ops.segment_sum(prod, models, num_segments=MB_COL)
        return (carry + jax.vmap(one_col)(panels_r, models_r, counts_r), None)
    start = jnp.zeros((N_COL, MB_COL, TILE), jnp.float32)
    total, _ = lax.scan(step, start, (tiles, tile_model, ray_counts, ray_half))
    return total

def reference(tiles, tile_model, ray_counts, data):
    beta = jnp.sqrt(jnp.sum(data * data) + EPS)
    u = data / beta
    v = backward(tiles, tile_model, ray_counts, u.astype(jnp.bfloat16).reshape(N_ROW, RB_DEV, TILE))
    alpha = jnp.sqrt(jnp.sum(v * v) + EPS)
    v = v / alpha
    w = v
    x = jnp.zeros_like(v)
    phibar = beta
    rhobar = alpha
    for step_index in range(ITERS):
        u = forward(tiles, tile_model, ray_counts, v.astype(jnp.bfloat16)) - alpha * u
        beta = jnp.sqrt(jnp.sum(u * u) + EPS)
        u = u / beta
        v = backward(tiles, tile_model, ray_counts, u.astype(jnp.bfloat16).reshape(N_ROW, RB_DEV, TILE)) - beta * v
        alpha = jnp.sqrt(jnp.sum(v * v) + EPS)
        v = v / alpha
        rho = jnp.sqrt(rhobar * rhobar + beta * beta)
        cosine = rhobar / rho
        sine = beta / rho
        theta = sine * alpha
        rhobar = -cosine * alpha
        phi = cosine * phibar
        phibar = sine * phibar
        x = x + phi / rho * w
        w = v - theta / rho * w
    return (x.reshape(N_COL, MB_COL * TILE), u)
```

```python
import functools

import jax
import jax.numpy as jnp
from jax import lax
from jax.experimental import pallas as pl
from jax.experimental.pallas import tpu as pltpu
from jax.sharding import PartitionSpec as P

MESH = pl.DeviceIdType.MESH
EPS = 1e-06
F32, BF16, I32 = jnp.float32, jnp.bfloat16, jnp.int32
MB_DEV = 8
CORES = 2


def dot(a, b, contract=((1,), (0,))):
    return lax.dot_general(a, b, (contract, ((), ())), preferred_element_type=F32)


def iota(shape, axis):
    return lax.broadcasted_iota(I32, shape, axis)


def kernel(
    ny, nz, nx, slots, blocks, chunks,
    tiles_hbm, models, counts, data, model_out, ray_out,
    tiles, meta_src, meta, prod, pick, pick_t, own_sum, sib_src, sib_in, z_src, z_in,
    v_src, v_in, v_all, sel_src, sel_in, v_slots, z_sq_src, z_sq, y_sq_src, y_sq,
    x_src, x_in, fz_src, fz_in, fy_src, fy_in,
    tile_sem, s_meta, r_meta, s_prod, r_prod, s_sib, r_sib, s_z, r_z, s_v, r_v, s_va, r_va,
    s_sel, r_sel, s_zsq, r_zsq, s_ysq, r_ysq, s_x, r_x, s_fz, r_fz, s_fy, r_fy,
):
    edge = tiles.shape[-1]
    row, x = lax.axis_index("row"), lax.axis_index("col")
    c = lax.rem(row, CORES)
    z = lax.rem(row // CORES, nz)
    y = row // (CORES * nz)

    def wrap(value, size):
        return jnp.where(value >= size, value - size, value)

    def peer(dy=0, dz=0, dc=0, dx=0):
        y2, z2 = wrap(y + dy % ny, ny), wrap(z + dz % nz, nz)
        c2, x2 = wrap(c + dc, CORES), wrap(x + dx % nx, nx)
        return ((y2 * nz + z2) * CORES + c2, x2)

    def send(src, dst, s_sem, r_sem, target):
        copy = pltpu.make_async_remote_copy(
            src_ref=src, dst_ref=dst, send_sem=s_sem, recv_sem=r_sem, device_id=target, device_id_type=MESH
        )
        copy.start()
        return copy

    barrier = pltpu.get_barrier_semaphore()
    greeted = [peer(dc=1)]
    greeted += [peer(dy=d, dc=k) for d in range(1, ny) for k in range(CORES)]
    greeted += [peer(dz=d) for d in range(1, nz)]
    greeted += [peer(dx=d) for d in range(1, nx)]
    for target in greeted:
        pl.semaphore_signal(barrier, inc=1, device_id=target, device_id_type=MESH)

    step = slots // chunks
    loads = []
    for k in range(chunks):
        load = pltpu.make_async_copy(
            tiles_hbm.at[0, 0, pl.ds(k * step, step)], tiles.at[pl.ds(k * step, step)], tile_sem.at[k]
        )
        load.start()
        loads.append(load)

    count_row = counts[0].astype(F32)
    count_all = jnp.broadcast_to(count_row, (blocks, blocks))
    ahead = iota((blocks, blocks), 1) < iota((blocks, blocks), 0)
    first = jnp.sum(jnp.where(ahead, count_all, 0.0), axis=1, keepdims=True)
    upto = iota((blocks, blocks), 1) <= iota((blocks, blocks), 0)
    last = jnp.sum(jnp.where(upto, count_all, 0.0), axis=1, keepdims=True)
    first_w = jnp.broadcast_to(first, (blocks, edge))
    last_w = jnp.broadcast_to(last, (blocks, edge))
    slot_lane = iota((blocks, edge), 1).astype(F32)
    table = jnp.where((slot_lane >= first_w) & (slot_lane < last_w), 1.0, 0.0)
    used = jnp.sum(table, axis=0, keepdims=True)[:, :slots] > 0.5
    table_t = table.T[:slots].astype(BF16)

    ids = jnp.where(used, models[0].astype(F32), -1.0)
    none = jnp.full((1, edge - slots), -1.0, F32)
    d = data[...]
    d_sq = jnp.sum(d * d, axis=0, keepdims=True)
    rest = jnp.zeros((6, edge), F32)
    meta_src[0] = jnp.concatenate([jnp.concatenate([ids, none], axis=1), d_sq, rest], axis=0)
    meta_src[1] = jnp.concatenate([jnp.concatenate([none, ids], axis=1), d_sq, rest], axis=0)

    pl.semaphore_wait(barrier, len(greeted))

    sent = []
    meta_copies = [
        send(meta_src.at[k % 2], meta.at[k], s_meta.at[k], r_meta.at[k], peer(dy=k)) for k in range(1, ny)
    ]
    sent += meta_copies

    high = d.astype(BF16)
    low = (d - high.astype(F32)).astype(BF16)
    u_high, u_low = dot(table_t, high), dot(table_t, low)
    group = 8
    row_of = lax.rem(iota((2 * group, edge), 0), group)
    for k in range(chunks):
        loads[k].wait()
        for pair in range(step // (2 * group)):
            parts = []
            for half in range(2):
                base = k * step + (2 * pair + half) * group
                both = jnp.concatenate([u_high[base : base + group], u_low[base : base + group]], axis=0)
                left = jnp.concatenate(
                    [jnp.where(row_of == i, both, 0.0).astype(BF16) for i in range(group)], axis=1
                )
                right = tiles[base : base + group].reshape(group * edge, edge)
                out = dot(left, right)
                parts.append(out[:group] + out[group:])
            base = k * step + 2 * pair * group
            prod[0, base : base + 2 * group] = jnp.concatenate(parts, axis=0).astype(BF16)
    prod_copies = [
        send(prod.at[0], prod.at[k], s_prod.at[k], r_prod.at[k], peer(dy=k)) for k in range(1, ny)
    ]
    sent += prod_copies

    rows = nz * CORES * MB_DEV

    def block_of(r):
        dz = r // (CORES * MB_DEV)
        half = lax.rem(r // MB_DEV, CORES)
        z2 = wrap(dz + z, nz)
        c2 = wrap(half + c, CORES)
        return (((y * nz + z2) * CORES + c2) * MB_DEV + lax.rem(r, MB_DEV)).astype(F32)

    meta[0] = meta_src[0]
    for copy in meta_copies:
        copy.wait_recv()
    y_data_sq = meta[0, 1:2]
    for k in range(1, ny):
        y_data_sq = y_data_sq + meta[k, 1:2]
    z_sq_src[...] = jnp.broadcast_to(y_data_sq, z_sq_src.shape)
    zsq_copies = [
        send(z_sq_src, z_sq.at[k], s_zsq.at[k], r_zsq.at[k], peer(dz=k)) for k in range(1, nz)
    ]
    sent += zsq_copies
    id_rows = [jnp.maximum(meta[2 * p, 0:1], meta[2 * p + 1, 0:1]) for p in range(ny // 2)]
    block_col = block_of(iota((rows, edge), 0))
    for p in range(ny // 2):
        pick[:, p * edge : (p + 1) * edge] = jnp.where(block_col == id_rows[p], 1.0, 0.0).astype(BF16)
    id_cols = jnp.concatenate(id_rows + [none_row(edge)] * (8 - ny // 2), axis=0).T
    block_row = block_of(iota((edge, rows), 1))
    for p in range(ny // 2):
        pick_t[p * edge : (p + 1) * edge] = jnp.where(id_cols[:, p : p + 1] == block_row, 1.0, 0.0).astype(BF16)

    for copy in prod_copies:
        copy.wait_recv()
    sums = dot(pick[...], prod[...].reshape(ny * slots, edge)).reshape(nz, CORES, MB_DEV, edge)
    sib_src[...] = sums[:, 1]
    sib_copy = send(sib_src, sib_in, s_sib, r_sib, peer(dc=1))
    sent.append(sib_copy)
    own_sum[...] = sums[:, 0]
    z_data_sq = y_data_sq
    for k, copy in enumerate(zsq_copies):
        copy.wait_recv()
        z_data_sq = z_data_sq + z_sq[k + 1, 0:1]
    sib_copy.wait_recv()
    z_src[...] = own_sum[...] + sib_in[...]

    z_copies = [send(z_src.at[k], z_in.at[k], s_z.at[k], r_z.at[k], peer(dz=k)) for k in range(1, nz)]
    sent += z_copies
    v_own = z_src[0]
    for k, copy in enumerate(z_copies):
        copy.wait_recv()
        v_own = v_own + z_in[k + 1]

    v_src[0:MB_DEV] = v_own
    v_src[MB_DEV:] = jnp.broadcast_to(z_data_sq, (8, edge))
    v_copy = send(v_src, v_in, s_v, r_v, peer(dc=1))
    sent.append(v_copy)
    v_copy.wait_recv()
    data_sq = z_data_sq + v_in[MB_DEV : MB_DEV + 1]
    v_all[0] = jnp.concatenate([v_own, v_in[0:MB_DEV]], axis=0).astype(BF16)
    va_copies = [
        send(v_all.at[0], v_all.at[k], s_va.at[k], r_va.at[k], peer(dz=-k)) for k in range(1, nz)
    ]
    sent += va_copies
    for copy in va_copies:
        copy.wait_recv()
    v_y = v_all[...].reshape(rows, edge)
    sel_src[...] = dot(pick_t[...], v_y).astype(BF16).reshape(ny, slots, edge)
    sel_copies = [
        send(sel_src.at[k], sel_in.at[k], s_sel.at[k], r_sel.at[k], peer(dy=-k)) for k in range(1, ny)
    ]
    sent += sel_copies
    v_wide = v_y.astype(F32)
    y_norm = jnp.sum(v_wide * v_wide, axis=0, keepdims=True)
    y_sq_src[...] = jnp.broadcast_to(y_norm, y_sq_src.shape)
    ysq_copies = [
        send(y_sq_src, y_sq.at[k], s_ysq.at[k], r_ysq.at[k], peer(dy=k)) for k in range(1, ny)
    ]
    sent += ysq_copies
    total = sel_src[0].astype(F32)
    for k, copy in enumerate(sel_copies):
        copy.wait_recv()
        total = total + sel_in[k + 1].astype(F32)
    v_slots[...] = total

    acc = jnp.zeros((blocks, edge), F32)
    for t in range(slots):
        mine = (first_w <= float(t)) & (last_w > float(t))
        left = jnp.where(mine, jnp.broadcast_to(v_slots[t : t + 1], (blocks, edge)), 0.0).astype(BF16)
        acc = acc + dot(left, tiles[t], ((1,), (1,)))
    for k, copy in enumerate(ysq_copies):
        copy.wait_recv()
        y_norm = y_norm + y_sq[k + 1, 0:1]

    x_src[0:blocks] = acc
    x_src[blocks:] = jnp.broadcast_to(y_norm, (8, edge))
    x_copies = [send(x_src, x_in.at[k], s_x.at[k], r_x.at[k], peer(dx=k)) for k in range(1, nx)]
    sent += x_copies
    full = x_src[...]
    for k, copy in enumerate(x_copies):
        copy.wait_recv()
        full = full + x_in[k + 1]
    beta0 = jnp.sqrt(jnp.sum(data_sq, axis=1, keepdims=True) + EPS)
    v_sq = jnp.sum(full[blocks : blocks + 1], axis=1, keepdims=True)
    alpha = jnp.sqrt(v_sq / (beta0 * beta0) + EPS)
    u = full[0:blocks] * (1.0 / beta0 / alpha) - d * (alpha / beta0)
    part = jnp.sum(u * u, axis=0, keepdims=True)

    fz_src[...] = jnp.broadcast_to(part, fz_src.shape)
    fz_copies = [send(fz_src, fz_in.at[k], s_fz.at[k], r_fz.at[k], peer(dz=k)) for k in range(1, nz)]
    sent += fz_copies
    for k, copy in enumerate(fz_copies):
        copy.wait_recv()
        part = part + fz_in[k + 1, 0:1]
    fy_src[...] = jnp.broadcast_to(part, fy_src.shape)
    fy_copies = []
    for k in range(1, ny * CORES):
        fy_copies.append(
            send(fy_src, fy_in.at[k], s_fy.at[k], r_fy.at[k], peer(dy=k // CORES, dc=k % CORES))
        )
    sent += fy_copies
    for k, copy in enumerate(fy_copies):
        copy.wait_recv()
        part = part + fy_in[k + 1, 0:1]
    beta_sq = jnp.sum(part, axis=1, keepdims=True) + EPS
    ray_out[...] = u * (1.0 / jnp.sqrt(beta_sq))
    model_out[...] = v_own * (1.0 / (alpha * alpha + beta_sq))
    for copy in sent:
        copy.wait_send()


def none_row(edge):
    return jnp.full((1, edge), -1.0, F32)


def build(mesh, ny, nz, nx):
    def on_device(tiles, tile_model, ray_counts, data):
        slots, edge = tiles.shape[2], tiles.shape[3]
        blocks = ray_counts.shape[2]
        chunks = 4
        rows = nz * CORES * MB_DEV
        vmem, dma = pltpu.VMEM, pltpu.SemaphoreType.DMA
        model, rays = pl.pallas_call(
            functools.partial(kernel, ny, nz, nx, slots, blocks, chunks),
            out_shape=(
                jax.ShapeDtypeStruct((MB_DEV, edge), F32),
                jax.ShapeDtypeStruct((blocks, edge), F32),
            ),
            in_specs=[
                pl.BlockSpec(memory_space=pltpu.HBM),
                pl.BlockSpec(memory_space=pltpu.VMEM),
                pl.BlockSpec(memory_space=pltpu.VMEM),
                pl.BlockSpec(memory_space=pltpu.VMEM),
            ],
            out_specs=(pl.BlockSpec(memory_space=pltpu.VMEM), pl.BlockSpec(memory_space=pltpu.VMEM)),
            scratch_shapes=[
                vmem((slots, edge, edge), BF16),
                vmem((2, 8, edge), F32),
                vmem((ny, 8, edge), F32),
                vmem((ny, slots, edge), BF16),
                vmem((rows, ny * slots), BF16),
                vmem((ny * slots, rows), BF16),
                vmem((nz, MB_DEV, edge), F32),
                vmem((nz, MB_DEV, edge), F32),
                vmem((nz, MB_DEV, edge), F32),
                vmem((nz, MB_DEV, edge), F32),
                vmem((nz, MB_DEV, edge), F32),
                vmem((2 * MB_DEV, edge), F32),
                vmem((2 * MB_DEV, edge), F32),
                vmem((nz, 2 * MB_DEV, edge), BF16),
                vmem((ny, slots, edge), BF16),
                vmem((ny, slots, edge), BF16),
                vmem((slots, edge), F32),
                vmem((8, edge), F32),
                vmem((nz, 8, edge), F32),
                vmem((8, edge), F32),
                vmem((ny, 8, edge), F32),
                vmem((blocks + 8, edge), F32),
                vmem((nx, blocks + 8, edge), F32),
                vmem((8, edge), F32),
                vmem((nz, 8, edge), F32),
                vmem((8, edge), F32),
                vmem((ny * CORES, 8, edge), F32),
                dma((chunks,)),
                dma((ny,)), dma((ny,)),
                dma((ny,)), dma((ny,)),
                dma, dma,
                dma((nz,)), dma((nz,)),
                dma, dma,
                dma((nz,)), dma((nz,)),
                dma((ny,)), dma((ny,)),
                dma((nz,)), dma((nz,)),
                dma((ny,)), dma((ny,)),
                dma((nx,)), dma((nx,)),
                dma((nz,)), dma((nz,)),
                dma((ny * CORES,)), dma((ny * CORES,)),
            ],
            compiler_params=pltpu.CompilerParams(
                collective_id=0, has_side_effects=True, vmem_limit_bytes=32 * 1024 * 1024
            ),
        )(tiles, tile_model, ray_counts, data.reshape(blocks, edge))
        return model.reshape(1, -1), rays.reshape(-1)

    return jax.shard_map(
        on_device,
        mesh=mesh,
        in_specs=(
            P("row", "col", None, None, None),
            P("row", "col", None),
            P("row", "col", None),
            P("row"),
        ),
        out_specs=(P("col", "row"), P("row")),
        check_vma=False,
    )


def solution(mesh):
    nz = 12
    return build(mesh, mesh.shape["row"] // (CORES * nz), nz, mesh.shape["col"])
```

```python
import functools

import jax
import jax.numpy as jnp
from jax import lax
from jax.experimental import pallas as pl
from jax.experimental.pallas import tpu as pltpu
from jax.sharding import PartitionSpec as P

MESH = pl.DeviceIdType.MESH
EPS = 1e-06
F32, BF16, I32 = jnp.float32, jnp.bfloat16, jnp.int32
MB_DEV = 8
CORES = 2


def dot(a, b, contract=((1,), (0,))):
    return lax.dot_general(a, b, (contract, ((), ())), preferred_element_type=F32)


def iota(shape, axis):
    return lax.broadcasted_iota(I32, shape, axis)


def kernel(
    ny, nz, nx, slots, blocks, chunks, wide,
    tiles_hbm, models_hbm, counts_hbm, data_hbm, model_out, ray_out,
    tiles, models, counts, data, give_src, give, ask_src, ask, prod, match, picked,
    sel_src, sel_in, v_slots, x_src, x_in, f_in,
    tile_sem, in_sem, s_give, r_give, s_ask, r_ask, s_prod, r_prod, s_rel, r_rel,
    s_sel, r_sel, s_x, r_x, s_f, r_f,
):
    edge = tiles.shape[-1]
    row, x = lax.axis_index("row"), lax.axis_index("col")
    c = lax.rem(row, CORES)
    z = lax.rem(row // CORES, nz)
    y = row // (CORES * nz)

    def wrap(value, size):
        return jnp.where(value >= size, value - size, value)

    def peer(dy=0, dz=0, dc=0, dx=0):
        y2, z2 = wrap(y + dy % ny, ny), wrap(z + dz % nz, nz)
        c2, x2 = wrap(c + dc, CORES), wrap(x + dx % nx, nx)
        return ((y2 * nz + z2) * CORES + c2, x2)

    def far(size):
        return sorted(range(1, size), key=lambda k: -min(k, size - k))

    def send(src, dst, s_sem, r_sem, target):
        copy = pltpu.make_async_remote_copy(
            src_ref=src, dst_ref=dst, send_sem=s_sem, recv_sem=r_sem, device_id=target, device_id_type=MESH
        )
        copy.start()
        return copy

    barrier = pltpu.get_barrier_semaphore()
    greeted = [peer(dc=1)]
    greeted += [peer(dy=d) for d in range(1, ny)]
    greeted += [peer(dz=d, dc=k) for d in range(1, nz) for k in range(CORES)]
    greeted += [peer(dx=d, dc=k) for d in range(1, nx) for k in range(CORES)]
    for target in greeted:
        pl.semaphore_signal(barrier, inc=1, device_id=target, device_id_type=MESH)

    small = []
    for k, (src, dst) in enumerate(((counts_hbm, counts), (models_hbm, models), (data_hbm, data))):
        load = pltpu.make_async_copy(src, dst, in_sem.at[k])
        load.start()
        small.append(load)
    step = slots // chunks
    loads = []
    for k in range(chunks):
        load = pltpu.make_async_copy(
            tiles_hbm.at[0, 0, pl.ds(k * step, step)], tiles.at[pl.ds(k * step, step)], tile_sem.at[k]
        )
        load.start()
        loads.append(load)

    for load in small:
        load.wait()

    count_row = counts[0].astype(F32)
    count_all = jnp.broadcast_to(count_row, (blocks, blocks))
    ahead = iota((blocks, blocks), 1) < iota((blocks, blocks), 0)
    first = jnp.sum(jnp.where(ahead, count_all, 0.0), axis=1, keepdims=True)
    upto = iota((blocks, blocks), 1) <= iota((blocks, blocks), 0)
    last = jnp.sum(jnp.where(upto, count_all, 0.0), axis=1, keepdims=True)
    first_w = jnp.broadcast_to(first, (blocks, edge))
    last_w = jnp.broadcast_to(last, (blocks, edge))
    slot_lane = iota((blocks, edge), 1).astype(F32)
    table = jnp.where((slot_lane >= first_w) & (slot_lane < last_w), 1.0, 0.0)
    used = jnp.sum(table, axis=0, keepdims=True)[:, :slots] > 0.5
    table_t = table.T[:slots].astype(BF16)

    models_row = models[0].astype(F32)
    ids = jnp.where(used, models_row, -1.0)
    none = jnp.full((1, edge - slots), -1.0, F32)
    give_src[0:1] = jnp.concatenate([ids, none], axis=1)
    give_src[8:9] = jnp.concatenate([none, ids], axis=1)
    lane = iota((1, edge), 1)
    owned = jnp.where(lane < slots + MB_DEV, (row * MB_DEV + lane - slots).astype(F32), -2.0)
    asked = jnp.concatenate([jnp.where(used, models_row, -2.0), none], axis=1)
    ask_src[0:1] = jnp.where(lane < slots, asked, owned)
    d = data[...]

    high = d.astype(BF16)
    low = (d - high.astype(F32)).astype(BF16)
    u_high, u_low = dot(table_t, high), dot(table_t, low)
    group = 8
    row_of = lax.rem(iota((2 * group, edge), 0), group)
    for k in range(chunks):
        loads[k].wait()
        for pair in range(step // (2 * group)):
            parts = []
            for half in range(2):
                base = k * step + (2 * pair + half) * group
                both = jnp.concatenate([u_high[base : base + group], u_low[base : base + group]], axis=0)
                left = jnp.concatenate(
                    [jnp.where(row_of == i, both, 0.0).astype(BF16) for i in range(group)], axis=1
                )
                right = tiles[base : base + group].reshape(group * edge, edge)
                out = dot(left, right)
                parts.append(out[:group] + out[group:])
            base = k * step + 2 * pair * group
            prod[0, 0, 0, base : base + 2 * group] = jnp.concatenate(parts, axis=0).astype(BF16)

    order = [0] + [k for i in range(1, nz // 2 + 1) for k in ((i, nz - i) if 2 * i != nz else (i,))]
    place = {k: (order.index(k) // 2, order.index(k) % 2) for k in order}
    sent = []
    pl.semaphore_wait(barrier, len(greeted))
    ask_copies = [
        send(ask_src.at[0:1], ask.at[k : k + 1], s_ask.at[k], r_ask.at[k], peer(dy=k)) for k in far(ny)
    ]
    give_copies = []
    for k in far(nz) + [0]:
        for i in range(CORES):
            if k + i > 0:
                half, slot = 8 * place[k][1], i * nz + k
                give_copies.append(
                    send(
                        give_src.at[half : half + 1], give.at[slot : slot + 1],
                        s_give.at[slot], r_give.at[slot], peer(dz=k, dc=i),
                    )
                )
    prod_copies = {
        k: send(
            prod.at[0, 0, 0], prod.at[place[k][0], 0, place[k][1]], s_prod.at[k], r_prod.at[k], peer(dz=k)
        )
        for k in far(nz)
    }

    def relay(k):
        pair, j = place[k]
        return send(prod.at[pair, 0, j], prod.at[pair, 1, j], s_rel.at[k], r_rel.at[k], peer(dc=1))

    relays = {0: relay(0)}
    sent += ask_copies + give_copies + list(prod_copies.values())

    for copy in ask_copies:
        copy.wait_recv()
    ask[0:1] = ask_src[0:1]
    ask_cols = ask[...].T
    for copy in give_copies:
        copy.wait_recv()
    give[0:1] = give_src[0:1]
    for pair in range(nz // 2):
        for i in range(CORES):
            k0, k1 = i * nz + order[2 * pair], i * nz + order[2 * pair + 1]
            given = jnp.maximum(give[k0 : k0 + 1], give[k1 : k1 + 1])
            for p in range(ny):
                wanted = jnp.broadcast_to(ask_cols[0:wide, p : p + 1], (wide, edge))
                match[pair, p * wide : (p + 1) * wide, i * edge : (i + 1) * edge] = jnp.where(
                    wanted == given, 1.0, 0.0
                ).astype(BF16)

    def add(pair):
        for j in range(2):
            relays[order[2 * pair + j]].wait_recv()
        part = dot(match[pair], prod[pair].reshape(CORES * 2 * slots, edge))
        picked[...] = part if pair == 0 else picked[...] + part

    for pair in range(nz // 2):
        for j in range(2):
            k = order[2 * pair + j]
            if k > 0:
                prod_copies[k].wait_recv()
                relays[k] = relay(k)
        if pair > 0:
            add(pair - 1)
    add(nz // 2 - 1)
    sent += list(relays.values())

    sel_src[...] = picked[...].astype(BF16).reshape(ny, wide, edge)
    sel_copies = [
        send(sel_src.at[k], sel_in.at[k], s_sel.at[k], r_sel.at[k], peer(dy=-k)) for k in far(ny)
    ]
    sent += sel_copies
    total = picked[0:wide].astype(BF16).astype(F32)
    for copy in sel_copies:
        copy.wait_recv()
    for k in range(1, ny):
        total = total + sel_in[k].astype(F32)
    v_own = total[slots : slots + MB_DEV]
    v_slots[...] = total[0:slots]

    acc = jnp.zeros((blocks, edge), F32)
    for t in range(slots):
        mine = (first_w <= float(t)) & (last_w > float(t))
        left = jnp.where(mine, jnp.broadcast_to(v_slots[t : t + 1], (blocks, edge)), 0.0).astype(BF16)
        acc = acc + dot(left, tiles[t], ((1,), (1,)))

    def over_rows(value):
        return jnp.sum(value, axis=0, keepdims=True)

    x_src[0:blocks] = acc
    terms = [over_rows(v_own * v_own), over_rows(acc * d), over_rows(d * d)]
    x_src[blocks:] = jnp.concatenate(terms + [jnp.zeros((8 - len(terms), edge), F32)], axis=0)
    rows = pl.ds(0, blocks + len(terms))
    x_copies = [
        send(x_src.at[rows], x_in.at[nx * i + k, rows], s_x.at[nx * i + k], r_x.at[nx * i + k], peer(dx=k, dc=i))
        for k in far(nx) + [0]
        for i in range(CORES)
        if k + i > 0
    ]
    sent += x_copies
    for copy in x_copies:
        copy.wait_recv()
    own, other = x_src[0 : blocks + 2], x_in[nx, 0 : blocks + 2]
    for k in range(1, nx):
        own = own + x_in[k, 0 : blocks + 2]
        other = other + x_in[nx + k, 0 : blocks + 2]
    g = own[0:blocks]
    g_other = other[0:blocks]
    v_row = own[blocks : blocks + 1] + other[blocks : blocks + 1]
    gd_row = own[blocks + 1 : blocks + 2] + other[blocks + 1 : blocks + 2]
    d_row = x_src[blocks + 2 : blocks + 3] + x_in[nx, blocks + 2 : blocks + 3]
    g_row = over_rows(g * g + g_other * g_other)

    quarter = edge // 4
    stack = jnp.concatenate([g_row, gd_row, d_row, v_row, jnp.zeros((4, edge), F32)], axis=0)
    stack = stack + pltpu.roll(stack, 2 * quarter, 1)
    stack = stack + pltpu.roll(stack, quarter, 1)
    mine = iota((8, edge), 1) // quarter == iota((8, edge), 0)
    f_in[0:1] = over_rows(jnp.where(mine, stack, 0.0))
    f_copies = []
    for i in far(ny) + [0]:
        for k in far(nz) + [0]:
            slot = i * nz + k
            if slot > 0:
                f_copies.append(
                    send(f_in.at[0:1], f_in.at[slot : slot + 1], s_f.at[slot], r_f.at[slot], peer(dy=i, dz=k))
                )
    sent += f_copies
    for copy in f_copies:
        copy.wait_recv()
    sums = jnp.broadcast_to(over_rows(f_in[...]), (8, edge))
    sums = jnp.sum(jnp.where(mine, sums, 0.0), axis=1, keepdims=True)
    g_sq, gd, d_sq, v_sq = sums[0:1], sums[1:2], sums[2:3], sums[3:4]
    beta0_sq = d_sq + EPS
    beta0 = jnp.sqrt(beta0_sq)
    alpha_sq = v_sq / beta0_sq + EPS
    alpha = jnp.sqrt(alpha_sq)
    scale = 1.0 / (beta0 * alpha)
    u_sq = g_sq * (scale * scale) - (2.0 / beta0_sq) * gd + (alpha_sq / beta0_sq) * d_sq
    beta_sq = jnp.maximum(u_sq, 0.0) + EPS
    back = 1.0 / jnp.sqrt(beta_sq)
    ray_out[...] = g * (scale * back) - d * (alpha / beta0 * back)
    model_out[...] = v_own * (1.0 / (alpha_sq + beta_sq))
    for copy in sent:
        copy.wait_send()


def build(mesh, ny, nz, nx):
    def on_device(tiles, tile_model, ray_counts, data):
        slots, edge = tiles.shape[2], tiles.shape[3]
        blocks = ray_counts.shape[2]
        chunks = 4
        wide = slots + 16
        rows = ny * wide
        vmem, dma = pltpu.VMEM, pltpu.SemaphoreType.DMA
        model, rays = pl.pallas_call(
            functools.partial(kernel, ny, nz, nx, slots, blocks, chunks, wide),
            out_shape=(
                jax.ShapeDtypeStruct((MB_DEV, edge), F32),
                jax.ShapeDtypeStruct((blocks, edge), F32),
            ),
            in_specs=[
                pl.BlockSpec(memory_space=pl.ANY),
                pl.BlockSpec(memory_space=pl.ANY),
                pl.BlockSpec(memory_space=pl.ANY),
                pl.BlockSpec(memory_space=pl.ANY),
            ],
            out_specs=(pl.BlockSpec(memory_space=pltpu.VMEM), pl.BlockSpec(memory_space=pltpu.VMEM)),
            scratch_shapes=[
                vmem((slots, edge, edge), BF16),
                vmem(tile_model.shape, I32),
                vmem(ray_counts.shape, I32),
                vmem((blocks, edge), F32),
                vmem((16, edge), F32),
                vmem((CORES * nz, edge), F32),
                vmem((8, edge), F32),
                vmem((ny, edge), F32),
                vmem((nz // 2, CORES, 2, slots, edge), BF16),
                vmem((nz // 2, rows, CORES * 2 * slots), BF16),
                vmem((rows, edge), F32),
                vmem((ny, wide, edge), BF16),
                vmem((ny, wide, edge), BF16),
                vmem((slots, edge), F32),
                vmem((blocks + 8, edge), F32),
                vmem((CORES * nx, blocks + 8, edge), F32),
                vmem((ny * nz, edge), F32),
                dma((chunks,)), dma((3,)),
                dma((CORES * nz,)), dma((CORES * nz,)),
                dma((ny,)), dma((ny,)),
                dma((nz,)), dma((nz,)),
                dma((nz,)), dma((nz,)),
                dma((ny,)), dma((ny,)),
                dma((CORES * nx,)), dma((CORES * nx,)),
                dma((ny * nz,)), dma((ny * nz,)),
            ],
            compiler_params=pltpu.CompilerParams(
                collective_id=0, has_side_effects=True, vmem_limit_bytes=56 * 1024 * 1024
            ),
        )(tiles, tile_model, ray_counts, data.reshape(blocks, edge))
        return model.reshape(1, -1), rays.reshape(-1)

    return jax.shard_map(
        on_device,
        mesh=mesh,
        in_specs=(
            P("row", "col", None, None, None),
            P("row", "col", None),
            P("row", "col", None),
            P("row"),
        ),
        out_specs=(P("col", "row"), P("row")),
        check_vma=False,
    )


def solution(mesh):
    nz = 12
    return build(mesh, mesh.shape["row"] // (CORES * nz), nz, mesh.shape["col"])
```

```python
import functools

import jax
import jax.numpy as jnp
from jax import lax
from jax.experimental import pallas as pl
from jax.experimental.pallas import tpu as pltpu
from jax.sharding import PartitionSpec as P

MESH = pl.DeviceIdType.MESH
EPS = 1e-06
F32, BF16, I32 = jnp.float32, jnp.bfloat16, jnp.int32
MB_DEV = 8
CORES = 2


def dot(a, b, contract=((1,), (0,))):
    return lax.dot_general(a, b, (contract, ((), ())), preferred_element_type=F32)


def iota(shape, axis):
    return lax.broadcasted_iota(I32, shape, axis)


def kernel(
    ny, nz, nx, slots, blocks, chunks, wide,
    tiles_hbm, integers, data_hbm, model_out, ray_out,
    tiles, data, give_src, give, ask_src, ask, prod, match, picked,
    sel_src, sel_in, v_slots, x_src, x_in, f_in,
    tile_sem, in_sem, s_give, r_give, s_ask, r_ask, s_prod, r_prod, s_rel, r_rel,
    s_sel, r_sel, s_own, r_own, s_x, r_x, s_f, r_f,
):
    edge = tiles.shape[-1]
    row, x = lax.axis_index("row"), lax.axis_index("col")
    c = lax.rem(row, CORES)
    z = lax.rem(row // CORES, nz)
    y = row // (CORES * nz)

    def wrap(value, size):
        return jnp.where(value >= size, value - size, value)

    def peer(dy=0, dz=0, dc=0, dx=0):
        y2, z2 = wrap(y + dy % ny, ny), wrap(z + dz % nz, nz)
        c2, x2 = wrap(c + dc, CORES), wrap(x + dx % nx, nx)
        return ((y2 * nz + z2) * CORES + c2, x2)

    def far(size):
        return sorted(range(1, size), key=lambda k: -min(k, size - k))

    def send(src, dst, s_sem, r_sem, target):
        copy = pltpu.make_async_remote_copy(
            src_ref=src, dst_ref=dst, send_sem=s_sem, recv_sem=r_sem, device_id=target, device_id_type=MESH
        )
        copy.start()
        return copy

    data_load = pltpu.make_async_copy(data_hbm, data, in_sem)
    data_load.start()
    step = slots // chunks
    loads = []
    for k in range(chunks):
        load = pltpu.make_async_copy(
            tiles_hbm.at[0, 0, pl.ds(k * step, step)], tiles.at[pl.ds(k * step, step)], tile_sem.at[k]
        )
        load.start()
        loads.append(load)

    def group(ref, s_sem, r_sem):
        return pltpu.make_async_remote_copy(
            src_ref=ref, dst_ref=ref, send_sem=s_sem, recv_sem=r_sem, device_id=peer(dc=1), device_id_type=MESH
        )

    barrier = pltpu.get_barrier_semaphore()
    greeted = [peer(dz=d, dc=k) for d in far(nz) for k in range(CORES)]
    greeted += [peer(dy=d) for d in far(ny)]
    greeted += [peer(dx=d, dc=k) for d in far(nx) for k in range(CORES)]
    greeted += [peer(dc=1)]
    for target in greeted:
        pl.semaphore_signal(barrier, inc=1, device_id=target, device_id_type=MESH)

    count_row = integers[0].astype(F32)[:, slots : slots + blocks]
    count_all = jnp.broadcast_to(count_row, (blocks, blocks))
    ahead = iota((blocks, blocks), 1) < iota((blocks, blocks), 0)
    first = jnp.sum(jnp.where(ahead, count_all, 0.0), axis=1, keepdims=True)
    upto = iota((blocks, blocks), 1) <= iota((blocks, blocks), 0)
    last = jnp.sum(jnp.where(upto, count_all, 0.0), axis=1, keepdims=True)
    first_w = jnp.broadcast_to(first, (blocks, edge))
    last_w = jnp.broadcast_to(last, (blocks, edge))
    slot_lane = iota((blocks, edge), 1).astype(F32)
    table = jnp.where((slot_lane >= first_w) & (slot_lane < last_w), 1.0, 0.0)
    used = jnp.sum(table, axis=0, keepdims=True)[:, :slots] > 0.5
    table_t = table.T[:slots].astype(BF16)

    models_row = integers[0].astype(F32)[:, 0:slots]
    ids = jnp.where(used, models_row, -1.0)
    none = jnp.full((1, edge - slots), -1.0, F32)
    give_src[0:1] = jnp.concatenate([ids, none], axis=1)
    give_src[8:9] = jnp.concatenate([none, ids], axis=1)
    lane = iota((1, edge), 1)
    owned = jnp.where(lane < slots + MB_DEV, (row * MB_DEV + lane - slots).astype(F32), -2.0)
    asked = jnp.concatenate([jnp.where(used, models_row, -2.0), none], axis=1)
    ask_src[0:1] = jnp.where(lane < slots, asked, owned)
    data_load.wait()
    d = data[...]

    order = far(nz) + [0]
    place = {k: (order.index(k) // 2, order.index(k) % 2) for k in order}
    home = prod.at[place[0][0], 0, place[0][1]]

    high = d.astype(BF16)
    low = (d - high.astype(F32)).astype(BF16)
    u_high, u_low = dot(table_t, high), dot(table_t, low)
    eight = 8
    row_of = lax.rem(iota((2 * eight, edge), 0), eight)
    for k in range(chunks):
        loads[k].wait()
        for pair in range(step // (2 * eight)):
            parts = []
            for half in range(2):
                base = k * step + (2 * pair + half) * eight
                both = jnp.concatenate([u_high[base : base + eight], u_low[base : base + eight]], axis=0)
                left = jnp.concatenate(
                    [jnp.where(row_of == i, both, 0.0).astype(BF16) for i in range(eight)], axis=1
                )
                right = tiles[base : base + eight].reshape(eight * edge, edge)
                out = dot(left, right)
                parts.append(out[:eight] + out[eight:])
            base = k * step + 2 * pair * eight
            home[base : base + 2 * eight] = jnp.concatenate(parts, axis=0).astype(BF16)

    sent = []
    pl.semaphore_wait(barrier, len(greeted))
    for k in far(ny):
        send(ask_src.at[0:1], ask.at[k : k + 1], s_ask, r_ask, peer(dy=k))
    for k in far(nz) + [0]:
        for i in range(CORES):
            if k + i > 0:
                half, slot = 8 * place[k][1], i * nz + k
                send(
                    give_src.at[half : half + 1], give.at[slot : slot + 1], s_give, r_give, peer(dz=k, dc=i)
                )
    for k in far(nz):
        pair, j = place[k]
        send(home, prod.at[pair, 0, j], s_prod.at[pair], r_prod.at[pair], peer(dz=k))
    prods = [
        group(prod.at[pair, 0] if 2 * pair + 2 < nz else prod.at[pair, 0, 0], s_prod.at[pair], r_prod.at[pair])
        for pair in range(nz // 2)
    ]
    asks = group(ask.at[1:ny], s_ask, r_ask)
    gives = group(give.at[1 : CORES * nz], s_give, r_give)
    relays = [group(prod.at[pair, 1], s_rel, r_rel.at[pair]) for pair in range(nz // 2)]
    relayed = group(prod.at[:, 0], s_rel, r_rel.at[0])

    def relay(k):
        pair, j = place[k]
        send(prod.at[pair, 0, j], prod.at[pair, 1, j], s_rel, r_rel.at[pair], peer(dc=1))

    relay(0)
    sent += [asks, gives, relayed] + prods

    asks.wait_recv()
    ask[0:1] = ask_src[0:1]
    ask_cols = ask[...].T
    gives.wait_recv()
    half = 8 * place[0][1]
    give[0:1] = give_src[half : half + 1]
    for pair in range(nz // 2):
        for i in range(CORES):
            k0, k1 = i * nz + order[2 * pair], i * nz + order[2 * pair + 1]
            given = jnp.maximum(give[k0 : k0 + 1], give[k1 : k1 + 1])
            for p in range(ny):
                wanted = jnp.broadcast_to(ask_cols[0:wide, p : p + 1], (wide, edge))
                match[pair, p * wide : (p + 1) * wide, i * edge : (i + 1) * edge] = jnp.where(
                    wanted == given, 1.0, 0.0
                ).astype(BF16)

    def add(pair):
        relays[pair].wait_recv()
        part = dot(match[pair], prod[pair].reshape(CORES * 2 * slots, edge))
        picked[...] = part if pair == 0 else picked[...] + part

    for pair in range(nz // 2):
        prods[pair].wait_recv()
        for k in order[2 * pair : 2 * pair + 2]:
            if k > 0:
                relay(k)
        if pair > 0:
            add(pair - 1)
    add(nz // 2 - 1)

    sel_src[...] = picked[...].astype(BF16).reshape(ny, wide, edge)
    slot_rows, own_rows = pl.ds(0, slots), pl.ds(slots, wide - slots)
    for k in far(ny):
        send(sel_src.at[k, slot_rows], sel_in.at[k, slot_rows], s_sel, r_sel, peer(dy=-k))
    for k in far(ny):
        send(sel_src.at[k, own_rows], sel_in.at[k, own_rows], s_own, r_own, peer(dy=-k))
    sels = group(sel_in.at[1:ny, slot_rows], s_sel, r_sel)
    owns = group(sel_in.at[1:ny, own_rows], s_own, r_own)
    sent += [sels, owns]
    total = picked[0:slots].astype(BF16).astype(F32)
    sels.wait_recv()
    for k in range(1, ny):
        total = total + sel_in[k, 0:slots].astype(F32)
    v_slots[...] = total

    acc = jnp.zeros((blocks, edge), F32)
    for base in range(0, slots, eight):
        left, right = [], []
        for t in range(base, base + eight):
            mine = (first_w <= float(t)) & (last_w > float(t))
            left.append(
                jnp.where(mine, jnp.broadcast_to(v_slots[t : t + 1], (blocks, edge)), 0.0).astype(BF16)
            )
            right.append(tiles[t])
        acc = acc + dot(jnp.concatenate(left, axis=1), jnp.concatenate(right, axis=1), ((1,), (1,)))
    v_own = picked[slots : slots + MB_DEV].astype(BF16).astype(F32)
    owns.wait_recv()
    for k in range(1, ny):
        v_own = v_own + sel_in[k, slots:wide].astype(F32)[0:MB_DEV]

    def over_rows(value):
        return jnp.sum(value, axis=0, keepdims=True)

    x_src[0:blocks] = acc
    terms = [over_rows(v_own * v_own), over_rows(acc * d), over_rows(d * d)]
    x_src[blocks:] = jnp.concatenate(terms + [jnp.zeros((8 - len(terms), edge), F32)], axis=0)
    rows = pl.ds(0, blocks + len(terms))
    for k in far(nx) + [0]:
        for i in range(CORES):
            if k + i > 0:
                send(x_src.at[rows], x_in.at[nx * i + k, rows], s_x, r_x, peer(dx=k, dc=i))
    over_x = group(x_in.at[1 : CORES * nx, rows], s_x, r_x)
    sent.append(over_x)
    over_x.wait_recv()
    own, other = x_src[0 : blocks + 2], x_in[nx, 0 : blocks + 2]
    for k in range(1, nx):
        own = own + x_in[k, 0 : blocks + 2]
        other = other + x_in[nx + k, 0 : blocks + 2]
    g = own[0:blocks]
    g_other = other[0:blocks]
    v_row = own[blocks : blocks + 1] + other[blocks : blocks + 1]
    gd_row = own[blocks + 1 : blocks + 2] + other[blocks + 1 : blocks + 2]
    d_row = x_src[blocks + 2 : blocks + 3] + x_in[nx, blocks + 2 : blocks + 3]
    g_row = over_rows(g * g + g_other * g_other)

    quarter = edge // 4
    stack = jnp.concatenate([g_row, gd_row, d_row, v_row, jnp.zeros((4, edge), F32)], axis=0)
    stack = stack + pltpu.roll(stack, 2 * quarter, 1)
    stack = stack + pltpu.roll(stack, quarter, 1)
    mine = iota((8, edge), 1) // quarter == iota((8, edge), 0)
    f_in[0:1] = over_rows(jnp.where(mine, stack, 0.0))
    for i in far(ny) + [0]:
        for k in far(nz) + [0]:
            slot = i * nz + k
            if slot > 0:
                send(f_in.at[0:1], f_in.at[slot : slot + 1], s_f, r_f, peer(dy=i, dz=k))
    finals = group(f_in.at[1 : ny * nz], s_f, r_f)
    sent.append(finals)
    for stage in sent:
        stage.wait_send()
    finals.wait_recv()
    sums = jnp.broadcast_to(over_rows(f_in[...]), (8, edge))
    sums = jnp.sum(jnp.where(mine, sums, 0.0), axis=1, keepdims=True)
    g_sq, gd, d_sq, v_sq = sums[0:1], sums[1:2], sums[2:3], sums[3:4]
    beta0_sq = d_sq + EPS
    beta0 = jnp.sqrt(beta0_sq)
    alpha_sq = v_sq / beta0_sq + EPS
    alpha = jnp.sqrt(alpha_sq)
    scale = 1.0 / (beta0 * alpha)
    u_sq = g_sq * (scale * scale) - (2.0 / beta0_sq) * gd + (alpha_sq / beta0_sq) * d_sq
    beta_sq = jnp.maximum(u_sq, 0.0) + EPS
    back = 1.0 / jnp.sqrt(beta_sq)
    ray_out[...] = g * (scale * back) - d * (alpha / beta0 * back)
    model_out[...] = v_own * (1.0 / (alpha_sq + beta_sq))


def build(mesh, ny, nz, nx):
    def on_device(tiles, tile_model, ray_counts, data):
        slots, edge = tiles.shape[2], tiles.shape[3]
        blocks = ray_counts.shape[2]
        chunks = 4
        wide = slots + 16
        rows = ny * wide
        integers = jnp.pad(tile_model, ((0, 0), (0, 0), (0, edge - slots))) + jnp.pad(
            ray_counts, ((0, 0), (0, 0), (slots, edge - slots - blocks))
        )
        vmem, dma = pltpu.VMEM, pltpu.SemaphoreType.DMA
        model, rays = pl.pallas_call(
            functools.partial(kernel, ny, nz, nx, slots, blocks, chunks, wide),
            out_shape=(
                jax.ShapeDtypeStruct((MB_DEV, edge), F32),
                jax.ShapeDtypeStruct((blocks, edge), F32),
            ),
            in_specs=[
                pl.BlockSpec(memory_space=pl.ANY),
                pl.BlockSpec(memory_space=pltpu.VMEM),
                pl.BlockSpec(memory_space=pl.ANY),
            ],
            out_specs=(pl.BlockSpec(memory_space=pltpu.VMEM), pl.BlockSpec(memory_space=pltpu.VMEM)),
            scratch_shapes=[
                vmem((slots, edge, edge), BF16),
                vmem((blocks, edge), F32),
                vmem((16, edge), F32),
                vmem((CORES * nz, edge), F32),
                vmem((8, edge), F32),
                vmem((ny, edge), F32),
                vmem((nz // 2, CORES, 2, slots, edge), BF16),
                vmem((nz // 2, rows, CORES * 2 * slots), BF16),
                vmem((rows, edge), F32),
                vmem((ny, wide, edge), BF16),
                vmem((ny, wide, edge), BF16),
                vmem((slots, edge), F32),
                vmem((blocks + 8, edge), F32),
                vmem((CORES * nx, blocks + 8, edge), F32),
                vmem((ny * nz, edge), F32),
                dma((chunks,)), dma,
                dma, dma,
                dma, dma,
                dma((nz // 2,)), dma((nz // 2,)),
                dma, dma((nz // 2,)),
                dma, dma,
                dma, dma,
                dma, dma,
                dma, dma,
            ],
            compiler_params=pltpu.CompilerParams(
                collective_id=0, has_side_effects=True, vmem_limit_bytes=55212 * 1024
            ),
        )(tiles, integers, data.reshape(blocks, edge))
        return model.reshape(1, -1), rays.reshape(-1)

    return jax.shard_map(
        on_device,
        mesh=mesh,
        in_specs=(
            P("row", "col", None, None, None),
            P("row", "col", None),
            P("row", "col", None),
            P("row"),
        ),
        out_specs=(P("col", "row"), P("row")),
        check_vma=False,
    )


def solution(mesh):
    nz = 12
    return build(mesh, mesh.shape["row"] // (CORES * nz), nz, mesh.shape["col"])
```

```python
import functools

import jax
import jax.numpy as jnp
from jax import lax
from jax.experimental import pallas as pl
from jax.experimental.pallas import tpu as pltpu
from jax.sharding import PartitionSpec as P

MESH = pl.DeviceIdType.MESH
EPS = 1e-06
F32, BF16, I32 = jnp.float32, jnp.bfloat16, jnp.int32
MB_DEV = 8
CORES = 2


def dot(a, b, contract=((1,), (0,))):
    return lax.dot_general(a, b, (contract, ((), ())), preferred_element_type=F32)


def iota(shape, axis):
    return lax.broadcasted_iota(I32, shape, axis)


def kernel(
    ny, nz, nx, slots, blocks, chunks, wide,
    tiles_hbm, integers, data_hbm, model_out, ray_out,
    tiles, data, give_src, give, give_in, ask_src, ask, prod, match, picked,
    sel_src, sel_in, v_slots, x_src, x_in, f_in,
    tile_sem, in_sem, s_give, r_give, s_give2, r_give2, s_ask, r_ask, s_prod, r_prod, s_rel, r_rel,
    s_sel, r_sel, s_own, r_own, s_x, r_x, s_f, r_f,
):
    edge = tiles.shape[-1]
    row, x = lax.axis_index("row"), lax.axis_index("col")
    c = lax.rem(row, CORES)
    z = lax.rem(row // CORES, nz)
    y = row // (CORES * nz)

    def wrap(value, size):
        return jnp.where(value >= size, value - size, value)

    def peer(dy=0, dz=0, dc=0, dx=0):
        y2, z2 = wrap(y + dy % ny, ny), wrap(z + dz % nz, nz)
        c2, x2 = wrap(c + dc, CORES), wrap(x + dx % nx, nx)
        return ((y2 * nz + z2) * CORES + c2, x2)

    def far(size):
        return sorted(range(1, size), key=lambda k: -min(k, size - k))

    def send(src, dst, s_sem, r_sem, target):
        copy = pltpu.make_async_remote_copy(
            src_ref=src, dst_ref=dst, send_sem=s_sem, recv_sem=r_sem, device_id=target, device_id_type=MESH
        )
        copy.start()
        return copy

    data_load = pltpu.make_async_copy(data_hbm, data, in_sem)
    data_load.start()
    step = slots // chunks
    loads = []
    for k in range(chunks):
        load = pltpu.make_async_copy(
            tiles_hbm.at[0, 0, pl.ds(k * step, step)], tiles.at[pl.ds(k * step, step)], tile_sem.at[k]
        )
        load.start()
        loads.append(load)

    def group(ref, s_sem, r_sem):
        return pltpu.make_async_remote_copy(
            src_ref=ref, dst_ref=ref, send_sem=s_sem, recv_sem=r_sem, device_id=peer(dc=1), device_id_type=MESH
        )

    barrier = pltpu.get_barrier_semaphore()
    greeted = [peer(dz=d) for d in far(nz)]
    greeted += [peer(dy=d) for d in far(ny)]
    greeted += [peer(dx=d, dc=k) for d in far(nx) for k in range(CORES)]
    greeted += [peer(dc=1)]
    for target in greeted:
        pl.semaphore_signal(barrier, inc=1, device_id=target, device_id_type=MESH)

    count_row = integers[0].astype(F32)[:, slots : slots + blocks]
    count_all = jnp.broadcast_to(count_row, (blocks, blocks))
    ahead = iota((blocks, blocks), 1) < iota((blocks, blocks), 0)
    first = jnp.sum(jnp.where(ahead, count_all, 0.0), axis=1, keepdims=True)
    upto = iota((blocks, blocks), 1) <= iota((blocks, blocks), 0)
    last = jnp.sum(jnp.where(upto, count_all, 0.0), axis=1, keepdims=True)
    first_w = jnp.broadcast_to(first, (blocks, edge))
    last_w = jnp.broadcast_to(last, (blocks, edge))
    slot_lane = iota((blocks, edge), 1).astype(F32)
    table = jnp.where((slot_lane >= first_w) & (slot_lane < last_w), 1.0, 0.0)
    used = jnp.sum(table, axis=0, keepdims=True)[:, :slots] > 0.5
    table_t = table.T[:slots].astype(BF16)

    models_row = integers[0].astype(F32)[:, 0:slots]
    ids = jnp.where(used, models_row, -1.0)
    none = jnp.full((1, edge - slots), -1.0, F32)
    give_src[0:1] = jnp.concatenate([ids, none], axis=1)
    give_src[8:9] = jnp.concatenate([none, ids], axis=1)
    lane = iota((1, edge), 1)
    owned = jnp.where(lane < slots + MB_DEV, (row * MB_DEV + lane - slots).astype(F32), -2.0)
    asked = jnp.concatenate([jnp.where(used, models_row, -2.0), none], axis=1)
    ask_src[0:1] = jnp.where(lane < slots, asked, owned)
    data_load.wait()
    d = data[...]

    order = far(nz) + [0]
    place = {k: (order.index(k) // 2, order.index(k) % 2) for k in order}
    home = prod.at[place[0][0], 0, place[0][1]]

    high = d.astype(BF16)
    low = (d - high.astype(F32)).astype(BF16)
    u_high, u_low = dot(table_t, high), dot(table_t, low)
    eight = 8
    row_of = lax.rem(iota((2 * eight, edge), 0), eight)
    for k in range(chunks):
        loads[k].wait()
        for pair in range(step // (2 * eight)):
            parts = []
            for half in range(2):
                base = k * step + (2 * pair + half) * eight
                both = jnp.concatenate([u_high[base : base + eight], u_low[base : base + eight]], axis=0)
                left = jnp.concatenate(
                    [jnp.where(row_of == i, both, 0.0).astype(BF16) for i in range(eight)], axis=1
                )
                right = tiles[base : base + eight].reshape(eight * edge, edge)
                out = dot(left, right)
                parts.append(out[:eight] + out[eight:])
            base = k * step + 2 * pair * eight
            home[base : base + 2 * eight] = jnp.concatenate(parts, axis=0).astype(BF16)

    sent = []
    pl.semaphore_wait(barrier, len(greeted))
    for k in far(ny):
        send(ask_src.at[0:1], ask.at[k : k + 1], s_ask, r_ask, peer(dy=k))
    for k in far(nz):
        half = 8 * place[k][1]
        send(give_src.at[half : half + 1], give.at[k : k + 1], s_give, r_give, peer(dz=k))
    for k in far(nz):
        pair, j = place[k]
        send(home, prod.at[pair, 0, j], s_prod.at[pair], r_prod.at[pair], peer(dz=k))
    prods = [
        group(prod.at[pair, 0] if 2 * pair + 2 < nz else prod.at[pair, 0, 0], s_prod.at[pair], r_prod.at[pair])
        for pair in range(nz // 2)
    ]
    asks = group(ask.at[1:ny], s_ask, r_ask)
    gives = group(give.at[1:nz], s_give, r_give)
    relays = [group(prod.at[pair, 1], s_rel, r_rel.at[pair]) for pair in range(nz // 2)]
    relayed = group(prod.at[:, 0], s_rel, r_rel.at[0])

    def relay(k):
        pair, j = place[k]
        send(prod.at[pair, 0, j], prod.at[pair, 1, j], s_rel, r_rel.at[pair], peer(dc=1))

    relay(0)
    sent += [asks, gives, relayed] + prods

    half = 8 * place[0][1]
    give[0:1] = give_src[half : half + 1]
    gives.wait_recv()
    other_gives = send(give.at[0:nz], give_in, s_give2, r_give2, peer(dc=1))
    sent.append(other_gives)
    asks.wait_recv()
    ask[0:1] = ask_src[0:1]
    ask_cols = ask[...].T
    other_gives.wait_recv()
    for pair in range(nz // 2):
        for i in range(CORES):
            k0, k1 = order[2 * pair], order[2 * pair + 1]
            table = (give, give_in)[i]
            given = jnp.maximum(table[k0 : k0 + 1], table[k1 : k1 + 1])
            for p in range(ny):
                wanted = jnp.broadcast_to(ask_cols[0:wide, p : p + 1], (wide, edge))
                match[pair, p * wide : (p + 1) * wide, i * edge : (i + 1) * edge] = jnp.where(
                    wanted == given, 1.0, 0.0
                ).astype(BF16)

    def add(pair):
        relays[pair].wait_recv()
        part = dot(match[pair], prod[pair].reshape(CORES * 2 * slots, edge))
        picked[...] = part if pair == 0 else picked[...] + part

    for pair in range(nz // 2):
        prods[pair].wait_recv()
        for k in order[2 * pair : 2 * pair + 2]:
            if k > 0:
                relay(k)
        if pair > 0:
            add(pair - 1)
    add(nz // 2 - 1)

    sel_src[...] = picked[...].astype(BF16).reshape(ny, wide, edge)
    slot_rows, own_rows = pl.ds(0, slots), pl.ds(slots, wide - slots)
    for k in far(ny):
        send(sel_src.at[k, slot_rows], sel_in.at[k, slot_rows], s_sel, r_sel, peer(dy=-k))
    for k in far(ny):
        send(sel_src.at[k, own_rows], sel_in.at[k, own_rows], s_own, r_own, peer(dy=-k))
    sels = group(sel_in.at[1:ny, slot_rows], s_sel, r_sel)
    owns = group(sel_in.at[1:ny, own_rows], s_own, r_own)
    sent += [sels, owns]
    total = picked[0:slots].astype(BF16).astype(F32)
    sels.wait_recv()
    for k in range(1, ny):
        total = total + sel_in[k, 0:slots].astype(F32)
    v_slots[...] = total

    acc = jnp.zeros((blocks, edge), F32)
    for base in range(0, slots, eight):
        left, right = [], []
        for t in range(base, base + eight):
            mine = (first_w <= float(t)) & (last_w > float(t))
            left.append(
                jnp.where(mine, jnp.broadcast_to(v_slots[t : t + 1], (blocks, edge)), 0.0).astype(BF16)
            )
            right.append(tiles[t])
        acc = acc + dot(jnp.concatenate(left, axis=1), jnp.concatenate(right, axis=1), ((1,), (1,)))
    v_own = picked[slots : slots + MB_DEV].astype(BF16).astype(F32)
    owns.wait_recv()
    v_own = v_own + jnp.sum(sel_in[1:ny, slots:wide].astype(F32), axis=0)[0:MB_DEV]

    def over_rows(value):
        return jnp.sum(value, axis=0, keepdims=True)

    x_src[0:blocks] = acc
    terms = [over_rows(v_own * v_own), over_rows(acc * d), over_rows(d * d)]
    x_src[blocks:] = jnp.concatenate(terms + [jnp.zeros((8 - len(terms), edge), F32)], axis=0)
    rows = pl.ds(0, blocks + len(terms))
    for k in far(nx) + [0]:
        for i in range(CORES):
            if k + i > 0:
                send(x_src.at[rows], x_in.at[nx * i + k, rows], s_x, r_x, peer(dx=k, dc=i))
    over_x = group(x_in.at[1 : CORES * nx, rows], s_x, r_x)
    sent.append(over_x)
    over_x.wait_recv()
    own, other = x_src[0 : blocks + 2], x_in[nx, 0 : blocks + 2]
    for k in range(1, nx):
        own = own + x_in[k, 0 : blocks + 2]
        other = other + x_in[nx + k, 0 : blocks + 2]
    g = own[0:blocks]
    g_other = other[0:blocks]
    v_row = own[blocks : blocks + 1] + other[blocks : blocks + 1]
    gd_row = own[blocks + 1 : blocks + 2] + other[blocks + 1 : blocks + 2]
    d_row = x_src[blocks + 2 : blocks + 3] + x_in[nx, blocks + 2 : blocks + 3]
    g_row = over_rows(g * g + g_other * g_other)

    quarter = edge // 4
    stack = jnp.concatenate([g_row, gd_row, d_row, v_row, jnp.zeros((4, edge), F32)], axis=0)
    stack = stack + pltpu.roll(stack, 2 * quarter, 1)
    stack = stack + pltpu.roll(stack, quarter, 1)
    mine = iota((8, edge), 1) // quarter == iota((8, edge), 0)
    f_in[0:1] = over_rows(jnp.where(mine, stack, 0.0))
    for i in far(ny) + [0]:
        for k in far(nz) + [0]:
            slot = i * nz + k
            if slot > 0:
                send(f_in.at[0:1], f_in.at[slot : slot + 1], s_f, r_f, peer(dy=i, dz=k))
    finals = group(f_in.at[1 : ny * nz], s_f, r_f)
    sent.append(finals)
    for stage in sent:
        stage.wait_send()
    finals.wait_recv()
    sums = jnp.broadcast_to(over_rows(f_in[...]), (8, edge))
    sums = jnp.sum(jnp.where(mine, sums, 0.0), axis=1, keepdims=True)
    g_sq, gd, d_sq, v_sq = sums[0:1], sums[1:2], sums[2:3], sums[3:4]
    beta0_sq = d_sq + EPS
    beta0 = jnp.sqrt(beta0_sq)
    alpha_sq = v_sq / beta0_sq + EPS
    alpha = jnp.sqrt(alpha_sq)
    scale = 1.0 / (beta0 * alpha)
    u_sq = g_sq * (scale * scale) - (2.0 / beta0_sq) * gd + (alpha_sq / beta0_sq) * d_sq
    beta_sq = jnp.maximum(u_sq, 0.0) + EPS
    back = 1.0 / jnp.sqrt(beta_sq)
    ray_out[...] = g * (scale * back) - d * (alpha / beta0 * back)
    model_out[...] = v_own * (1.0 / (alpha_sq + beta_sq))


def build(mesh, ny, nz, nx):
    def on_device(tiles, tile_model, ray_counts, data):
        slots, edge = tiles.shape[2], tiles.shape[3]
        blocks = ray_counts.shape[2]
        chunks = 4
        wide = slots + 16
        rows = ny * wide
        integers = jnp.pad(tile_model, ((0, 0), (0, 0), (0, edge - slots))) + jnp.pad(
            ray_counts, ((0, 0), (0, 0), (slots, edge - slots - blocks))
        )
        vmem, dma = pltpu.VMEM, pltpu.SemaphoreType.DMA
        model, rays = pl.pallas_call(
            functools.partial(kernel, ny, nz, nx, slots, blocks, chunks, wide),
            out_shape=(
                jax.ShapeDtypeStruct((MB_DEV, edge), F32),
                jax.ShapeDtypeStruct((blocks, edge), F32),
            ),
            in_specs=[
                pl.BlockSpec(memory_space=pl.ANY),
                pl.BlockSpec(memory_space=pltpu.VMEM),
                pl.BlockSpec(memory_space=pl.ANY),
            ],
            out_specs=(pl.BlockSpec(memory_space=pltpu.VMEM), pl.BlockSpec(memory_space=pltpu.VMEM)),
            scratch_shapes=[
                vmem((slots, edge, edge), BF16),
                vmem((blocks, edge), F32),
                vmem((16, edge), F32),
                vmem((nz, edge), F32),
                vmem((nz, edge), F32),
                vmem((8, edge), F32),
                vmem((ny, edge), F32),
                vmem((nz // 2, CORES, 2, slots, edge), BF16),
                vmem((nz // 2, rows, CORES * 2 * slots), BF16),
                vmem((rows, edge), F32),
                vmem((ny, wide, edge), BF16),
                vmem((ny, wide, edge), BF16),
                vmem((slots, edge), F32),
                vmem((blocks + 8, edge), F32),
                vmem((CORES * nx, blocks + 8, edge), F32),
                vmem((ny * nz, edge), F32),
                dma((chunks,)), dma,
                dma, dma, dma, dma,
                dma, dma,
                dma((nz // 2,)), dma((nz // 2,)),
                dma, dma((nz // 2,)),
                dma, dma,
                dma, dma,
                dma, dma,
                dma, dma,
            ],
            compiler_params=pltpu.CompilerParams(
                collective_id=0, has_side_effects=True, vmem_limit_bytes=55212 * 1024
            ),
        )(tiles, integers, data.reshape(blocks, edge))
        return model.reshape(1, -1), rays.reshape(-1)

    return jax.shard_map(
        on_device,
        mesh=mesh,
        in_specs=(
            P("row", "col", None, None, None),
            P("row", "col", None),
            P("row", "col", None),
            P("row"),
        ),
        out_specs=(P("col", "row"), P("row")),
        check_vma=False,
    )


def solution(mesh):
    nz = 12
    return build(mesh, mesh.shape["row"] // (CORES * nz), nz, mesh.shape["col"])
```

```python
import functools

import jax
import jax.numpy as jnp
from jax import lax
from jax.experimental import pallas as pl
from jax.experimental.pallas import tpu as pltpu
from jax.sharding import PartitionSpec as P

MESH = pl.DeviceIdType.MESH
EPS = 1e-06
F32, BF16, I32 = jnp.float32, jnp.bfloat16, jnp.int32
MB_DEV = 8
CORES = 2


def dot(a, b, contract=((1,), (0,))):
    return lax.dot_general(a, b, (contract, ((), ())), preferred_element_type=F32)


def iota(shape, axis):
    return lax.broadcasted_iota(I32, shape, axis)


def kernel(
    ny, nz, nx, slots, blocks, chunks, wide,
    tiles_hbm, integers, data_hbm, model_out, ray_out,
    tiles, turned, data, give_src, give, give_in, ask_src, ask, prod, match, picked,
    sel_src, sel_in, v_slots, x_src, x_in, f_in,
    tile_sem, in_sem, s_give, r_give, s_give2, r_give2, s_ask, r_ask, s_prod, r_prod, s_rel, r_rel,
    s_sel, r_sel, s_own, r_own, s_x, r_x, s_f, r_f,
):
    edge = tiles.shape[-1]
    row, x = lax.axis_index("row"), lax.axis_index("col")
    c = lax.rem(row, CORES)
    z = lax.rem(row // CORES, nz)
    y = row // (CORES * nz)

    def wrap(value, size):
        return jnp.where(value >= size, value - size, value)

    def peer(dy=0, dz=0, dc=0, dx=0):
        y2, z2 = wrap(y + dy % ny, ny), wrap(z + dz % nz, nz)
        c2, x2 = wrap(c + dc, CORES), wrap(x + dx % nx, nx)
        return ((y2 * nz + z2) * CORES + c2, x2)

    def far(size):
        return sorted(range(1, size), key=lambda k: -min(k, size - k))

    def send(src, dst, s_sem, r_sem, target):
        copy = pltpu.make_async_remote_copy(
            src_ref=src, dst_ref=dst, send_sem=s_sem, recv_sem=r_sem, device_id=target, device_id_type=MESH
        )
        copy.start()
        return copy

    def group(ref, s_sem, r_sem):
        return pltpu.make_async_remote_copy(
            src_ref=ref, dst_ref=ref, send_sem=s_sem, recv_sem=r_sem, device_id=peer(dc=1), device_id_type=MESH
        )

    barrier = pltpu.get_barrier_semaphore()
    greeted = [peer(dz=d) for d in far(nz)]
    greeted += [peer(dy=d) for d in far(ny)]
    greeted += [peer(dx=d, dc=k) for d in far(nx) for k in range(CORES)]
    greeted += [peer(dc=1)]
    for target in greeted:
        pl.semaphore_signal(barrier, inc=1, device_id=target, device_id_type=MESH)

    data_load = pltpu.make_async_copy(data_hbm, data, in_sem)
    data_load.start()
    step = slots // chunks
    loads = []
    for k in range(chunks):
        load = pltpu.make_async_copy(
            tiles_hbm.at[0, 0, pl.ds(k * step, step)], tiles.at[pl.ds(k * step, step)], tile_sem.at[k]
        )
        load.start()
        loads.append(load)

    count_row = integers[0].astype(F32)[:, slots : slots + blocks]
    count_all = jnp.broadcast_to(count_row, (blocks, blocks))
    ahead = iota((blocks, blocks), 1) < iota((blocks, blocks), 0)
    first = jnp.sum(jnp.where(ahead, count_all, 0.0), axis=1, keepdims=True)
    upto = iota((blocks, blocks), 1) <= iota((blocks, blocks), 0)
    last = jnp.sum(jnp.where(upto, count_all, 0.0), axis=1, keepdims=True)
    first_w = jnp.broadcast_to(first, (blocks, edge))
    last_w = jnp.broadcast_to(last, (blocks, edge))
    slot_lane = iota((blocks, edge), 1).astype(F32)
    table = jnp.where((slot_lane >= first_w) & (slot_lane < last_w), 1.0, 0.0)
    used = jnp.sum(table, axis=0, keepdims=True)[:, :slots] > 0.5
    table_t = table.T[:slots].astype(BF16)

    models_row = integers[0].astype(F32)[:, 0:slots]
    ids = jnp.where(used, models_row, -1.0)
    none = jnp.full((1, edge - slots), -1.0, F32)
    give_src[0:1] = jnp.concatenate([ids, none], axis=1)
    give_src[8:9] = jnp.concatenate([none, ids], axis=1)
    lane = iota((1, edge), 1)
    owned = jnp.where(lane < slots + MB_DEV, (row * MB_DEV + lane - slots).astype(F32), -2.0)
    asked = jnp.concatenate([jnp.where(used, models_row, -2.0), none], axis=1)
    ask_src[0:1] = jnp.where(lane < slots, asked, owned)
    data_load.wait()
    d = data[...]

    order = far(nz) + [0]
    place = {k: (order.index(k) // 2, order.index(k) % 2) for k in order}
    home = prod.at[place[0][0], 0, place[0][1]]

    high = d.astype(BF16)
    low = (d - high.astype(F32)).astype(BF16)
    u_high, u_low = dot(table_t, high), dot(table_t, low)
    eight = 8
    row_of = lax.rem(iota((2 * eight, edge), 0), eight)
    for k in range(chunks):
        loads[k].wait()
        for pair in range(step // (2 * eight)):
            parts = []
            for half in range(2):
                base = k * step + (2 * pair + half) * eight
                both = jnp.concatenate([u_high[base : base + eight], u_low[base : base + eight]], axis=0)
                left = jnp.concatenate(
                    [jnp.where(row_of == i, both, 0.0).astype(BF16) for i in range(eight)], axis=1
                )
                right = tiles[base : base + eight].reshape(eight * edge, edge)
                out = dot(left, right)
                parts.append(out[:eight] + out[eight:])
            base = k * step + 2 * pair * eight
            home[base : base + 2 * eight] = jnp.concatenate(parts, axis=0).astype(BF16)

    sent = []
    pl.semaphore_wait(barrier, len(greeted))
    for k in far(ny):
        send(ask_src.at[0:1], ask.at[k : k + 1], s_ask, r_ask, peer(dy=k))
    for k in far(nz):
        half = 8 * place[k][1]
        send(give_src.at[half : half + 1], give.at[k : k + 1], s_give, r_give, peer(dz=k))
    for k in far(nz):
        pair, j = place[k]
        send(home, prod.at[pair, 0, j], s_prod.at[pair], r_prod.at[pair], peer(dz=k))
    prods = [
        group(prod.at[pair, 0] if 2 * pair + 2 < nz else prod.at[pair, 0, 0], s_prod.at[pair], r_prod.at[pair])
        for pair in range(nz // 2)
    ]
    asks = group(ask.at[1:ny], s_ask, r_ask)
    gives = group(give.at[1:nz], s_give, r_give)
    relays = [group(prod.at[pair, 1], s_rel, r_rel.at[pair]) for pair in range(nz // 2)]
    relayed = group(prod.at[:, 0], s_rel, r_rel.at[0])

    def relay(k):
        pair, j = place[k]
        send(prod.at[pair, 0, j], prod.at[pair, 1, j], s_rel, r_rel.at[pair], peer(dc=1))

    relay(0)
    sent += [asks, gives, relayed] + prods

    for t in range(slots):
        turned[t] = tiles[t].T
    half = 8 * place[0][1]
    give[0:1] = give_src[half : half + 1]
    gives.wait_recv()
    other_gives = send(give.at[0:nz], give_in, s_give2, r_give2, peer(dc=1))
    sent.append(other_gives)
    per = nz // 4

    def fetch(part):
        for pair in range(part * per, (part + 1) * per):
            prods[pair].wait_recv()
            for k in order[2 * pair : 2 * pair + 2]:
                if k > 0:
                    relay(k)

    asks.wait_recv()
    ask[0:1] = ask_src[0:1]
    ask_cols = ask[...].T
    other_gives.wait_recv()
    for pair in range(nz // 2):
        for i in range(CORES):
            k0, k1 = order[2 * pair], order[2 * pair + 1]
            table = (give, give_in)[i]
            part, lanes = pair // per, (pair % per * CORES + i) * edge
            given = jnp.maximum(table[k0 : k0 + 1], table[k1 : k1 + 1])
            for p in range(ny):
                wanted = jnp.broadcast_to(ask_cols[0:wide, p : p + 1], (wide, edge))
                match[part, p * wide : (p + 1) * wide, lanes : lanes + edge] = jnp.where(
                    wanted == given, 1.0, 0.0
                ).astype(BF16)

    def add(part):
        pairs = slice(part * per, (part + 1) * per)
        for pair in range(part * per, (part + 1) * per):
            relays[pair].wait_recv()
        found = dot(match[part], prod[pairs].reshape(per * CORES * 2 * slots, edge))
        picked[...] = found if part == 0 else picked[...] + found

    fetch(0)
    fetch(1)
    add(0)
    add(1)

    sel_src[...] = picked[...].astype(BF16).reshape(ny, wide, edge)
    slot_rows, own_rows = pl.ds(0, slots), pl.ds(slots, wide - slots)
    for k in far(ny):
        send(sel_src.at[k, slot_rows], sel_in.at[k, slot_rows], s_sel, r_sel, peer(dy=-k))
    for k in far(ny):
        send(sel_src.at[k, own_rows], sel_in.at[k, own_rows], s_own, r_own, peer(dy=-k))
    sels = group(sel_in.at[1:ny, slot_rows], s_sel, r_sel)
    owns = group(sel_in.at[1:ny, own_rows], s_own, r_own)
    sent += [sels, owns]
    total = picked[0:slots].astype(BF16).astype(F32)
    sels.wait_recv()
    for k in range(1, ny):
        total = total + sel_in[k, 0:slots].astype(F32)
    v_slots[...] = total

    acc = jnp.zeros((blocks, edge), F32)
    for base in range(0, slots, eight):
        left = []
        for t in range(base, base + eight):
            mine = (first_w <= float(t)) & (last_w > float(t))
            left.append(
                jnp.where(mine, jnp.broadcast_to(v_slots[t : t + 1], (blocks, edge)), 0.0).astype(BF16)
            )
        acc = acc + dot(jnp.concatenate(left, axis=1), turned[base : base + eight].reshape(eight * edge, edge))
    v_own = picked[slots : slots + MB_DEV].astype(BF16).astype(F32)
    owns.wait_recv()
    v_own = v_own + jnp.sum(sel_in[1:ny, slots:wide].astype(F32), axis=0)[0:MB_DEV]

    def over_rows(value):
        return jnp.sum(value, axis=0, keepdims=True)

    x_src[0:blocks] = acc
    terms = [over_rows(v_own * v_own), over_rows(acc * d), over_rows(d * d)]
    x_src[blocks:] = jnp.concatenate(terms + [jnp.zeros((8 - len(terms), edge), F32)], axis=0)
    rows = pl.ds(0, blocks + len(terms))
    for k in far(nx) + [0]:
        for i in range(CORES):
            if k + i > 0:
                send(x_src.at[rows], x_in.at[nx * i + k, rows], s_x, r_x, peer(dx=k, dc=i))
    over_x = group(x_in.at[1 : CORES * nx, rows], s_x, r_x)
    sent.append(over_x)
    over_x.wait_recv()
    own, other = x_src[0 : blocks + 2], x_in[nx, 0 : blocks + 2]
    for k in range(1, nx):
        own = own + x_in[k, 0 : blocks + 2]
        other = other + x_in[nx + k, 0 : blocks + 2]
    g = own[0:blocks]
    g_other = other[0:blocks]
    v_row = own[blocks : blocks + 1] + other[blocks : blocks + 1]
    gd_row = own[blocks + 1 : blocks + 2] + other[blocks + 1 : blocks + 2]
    d_row = x_src[blocks + 2 : blocks + 3] + x_in[nx, blocks + 2 : blocks + 3]
    g_row = over_rows(g * g + g_other * g_other)

    quarter = edge // 4
    stack = jnp.concatenate([g_row, gd_row, d_row, v_row, jnp.zeros((4, edge), F32)], axis=0)
    stack = stack + pltpu.roll(stack, 2 * quarter, 1)
    stack = stack + pltpu.roll(stack, quarter, 1)
    mine = iota((8, edge), 1) // quarter == iota((8, edge), 0)
    f_in[0:1] = over_rows(jnp.where(mine, stack, 0.0))
    for i in far(ny) + [0]:
        for k in far(nz) + [0]:
            slot = i * nz + k
            if slot > 0:
                send(f_in.at[0:1], f_in.at[slot : slot + 1], s_f, r_f, peer(dy=i, dz=k))
    finals = group(f_in.at[1 : ny * nz], s_f, r_f)
    sent.append(finals)
    for stage in sent:
        stage.wait_send()
    finals.wait_recv()
    sums = jnp.broadcast_to(over_rows(f_in[...]), (8, edge))
    sums = jnp.sum(jnp.where(mine, sums, 0.0), axis=1, keepdims=True)
    g_sq, gd, d_sq, v_sq = sums[0:1], sums[1:2], sums[2:3], sums[3:4]
    beta0_sq = d_sq + EPS
    beta0 = jnp.sqrt(beta0_sq)
    alpha_sq = v_sq / beta0_sq + EPS
    alpha = jnp.sqrt(alpha_sq)
    scale = 1.0 / (beta0 * alpha)
    u_sq = g_sq * (scale * scale) - (2.0 / beta0_sq) * gd + (alpha_sq / beta0_sq) * d_sq
    beta_sq = jnp.maximum(u_sq, 0.0) + EPS
    back = 1.0 / jnp.sqrt(beta_sq)
    ray_out[...] = g * (scale * back) - d * (alpha / beta0 * back)
    model_out[...] = v_own * (1.0 / (alpha_sq + beta_sq))


def build(mesh, ny, nz, nx):
    def on_device(tiles, tile_model, ray_counts, data):
        slots, edge = tiles.shape[2], tiles.shape[3]
        blocks = ray_counts.shape[2]
        chunks = 4
        wide = slots + 16
        rows = ny * wide
        integers = jnp.pad(tile_model, ((0, 0), (0, 0), (0, edge - slots))) + jnp.pad(
            ray_counts, ((0, 0), (0, 0), (slots, edge - slots - blocks))
        )
        vmem, dma = pltpu.VMEM, pltpu.SemaphoreType.DMA
        model, rays = pl.pallas_call(
            functools.partial(kernel, ny, nz, nx, slots, blocks, chunks, wide),
            out_shape=(
                jax.ShapeDtypeStruct((MB_DEV, edge), F32),
                jax.ShapeDtypeStruct((blocks, edge), F32),
            ),
            in_specs=[
                pl.BlockSpec(memory_space=pl.ANY),
                pl.BlockSpec(memory_space=pltpu.VMEM),
                pl.BlockSpec(memory_space=pl.ANY),
            ],
            out_specs=(pl.BlockSpec(memory_space=pltpu.VMEM), pl.BlockSpec(memory_space=pltpu.VMEM)),
            scratch_shapes=[
                vmem((slots, edge, edge), BF16),
                vmem((slots, edge, edge), BF16),
                vmem((blocks, edge), F32),
                vmem((16, edge), F32),
                vmem((nz, edge), F32),
                vmem((nz, edge), F32),
                vmem((8, edge), F32),
                vmem((ny, edge), F32),
                vmem((nz // 2, CORES, 2, slots, edge), BF16),
                vmem((2, rows, nz // 2 * CORES * slots), BF16),
                vmem((rows, edge), F32),
                vmem((ny, wide, edge), BF16),
                vmem((ny, wide, edge), BF16),
                vmem((slots, edge), F32),
                vmem((blocks + 8, edge), F32),
                vmem((CORES * nx, blocks + 8, edge), F32),
                vmem((ny * nz, edge), F32),
                dma((chunks,)), dma,
                dma, dma, dma, dma,
                dma, dma,
                dma((nz // 2,)), dma((nz // 2,)),
                dma, dma((nz // 2,)),
                dma, dma,
                dma, dma,
                dma, dma,
                dma, dma,
            ],
            compiler_params=pltpu.CompilerParams(
                collective_id=0, has_side_effects=True, vmem_limit_bytes=55212 * 1024
            ),
        )(tiles, integers, data.reshape(blocks, edge))
        return model.reshape(1, -1), rays.reshape(-1)

    return jax.shard_map(
        on_device,
        mesh=mesh,
        in_specs=(
            P("row", "col", None, None, None),
            P("row", "col", None),
            P("row", "col", None),
            P("row"),
        ),
        out_specs=(P("col", "row"), P("row")),
        check_vma=False,
    )


def solution(mesh):
    nz = 12
    return build(mesh, mesh.shape["row"] // (CORES * nz), nz, mesh.shape["col"])
```

```python
import functools

import jax
import jax.numpy as jnp
from jax import lax
from jax.experimental import pallas as pl
from jax.experimental.pallas import tpu as pltpu
from jax.sharding import PartitionSpec as P

MESH = pl.DeviceIdType.MESH
EPS = 1e-06
F32, BF16, I32 = jnp.float32, jnp.bfloat16, jnp.int32
MB_DEV = 8
CORES = 2


def dot(a, b, contract=((1,), (0,))):
    return lax.dot_general(a, b, (contract, ((), ())), preferred_element_type=F32)


def iota(shape, axis):
    return lax.broadcasted_iota(I32, shape, axis)


def kernel(
    ny, nz, nx, slots, blocks, chunks, wide,
    tiles_hbm, integers, data_hbm, model_out, ray_out,
    tiles, turned, data, give_src, give, give_in, ask_src, ask, prod, match, picked,
    sel_src, sel_in, v_slots, x_src, x_in, f_in,
    tile_sem, in_sem, s_give, r_give, s_give2, r_give2, s_ask, r_ask, s_prod, r_prod, s_rel, r_rel,
    s_sel, r_sel, s_own, r_own, s_x, r_x, s_f, r_f,
):
    edge = tiles.shape[-1]
    row, x = lax.axis_index("row"), lax.axis_index("col")
    c = lax.rem(row, CORES)
    z = lax.rem(row // CORES, nz)
    y = row // (CORES * nz)

    def wrap(value, size):
        return jnp.where(value >= size, value - size, value)

    def peer(dy=0, dz=0, dc=0, dx=0):
        y2, z2 = wrap(y + dy % ny, ny), wrap(z + dz % nz, nz)
        c2, x2 = wrap(c + dc, CORES), wrap(x + dx % nx, nx)
        return ((y2 * nz + z2) * CORES + c2, x2)

    def far(size):
        return sorted(range(1, size), key=lambda k: -min(k, size - k))

    def send(src, dst, s_sem, r_sem, target):
        copy = pltpu.make_async_remote_copy(
            src_ref=src, dst_ref=dst, send_sem=s_sem, recv_sem=r_sem, device_id=target, device_id_type=MESH
        )
        copy.start()
        return copy

    def group(ref, s_sem, r_sem):
        return pltpu.make_async_remote_copy(
            src_ref=ref, dst_ref=ref, send_sem=s_sem, recv_sem=r_sem, device_id=peer(dc=1), device_id_type=MESH
        )

    barrier = pltpu.get_barrier_semaphore()
    greeted = [peer(dz=d) for d in far(nz)]
    greeted += [peer(dy=d) for d in far(ny)]
    greeted += [peer(dx=d, dc=k) for d in far(nx) for k in range(CORES)]
    greeted += [peer(dc=1)]
    for target in greeted:
        pl.semaphore_signal(barrier, inc=1, device_id=target, device_id_type=MESH)

    data_load = pltpu.make_async_copy(data_hbm, data, in_sem)
    data_load.start()
    step = slots // chunks
    loads = []
    for k in range(chunks):
        load = pltpu.make_async_copy(
            tiles_hbm.at[0, 0, pl.ds(k * step, step)], tiles.at[pl.ds(k * step, step)], tile_sem.at[k]
        )
        load.start()
        loads.append(load)

    count_row = integers[0].astype(F32)[:, slots : slots + blocks]
    count_all = jnp.broadcast_to(count_row, (blocks, blocks))
    ahead = iota((blocks, blocks), 1) < iota((blocks, blocks), 0)
    first = jnp.sum(jnp.where(ahead, count_all, 0.0), axis=1, keepdims=True)
    upto = iota((blocks, blocks), 1) <= iota((blocks, blocks), 0)
    last = jnp.sum(jnp.where(upto, count_all, 0.0), axis=1, keepdims=True)
    first_w = jnp.broadcast_to(first, (blocks, edge))
    last_w = jnp.broadcast_to(last, (blocks, edge))
    slot_lane = iota((blocks, edge), 1).astype(F32)
    table = jnp.where((slot_lane >= first_w) & (slot_lane < last_w), 1.0, 0.0)
    used = jnp.sum(table, axis=0, keepdims=True)[:, :slots] > 0.5
    table_t = table.T[:slots].astype(BF16)

    models_row = integers[0].astype(F32)[:, 0:slots]
    ids = jnp.where(used, models_row, -1.0)
    none = jnp.full((1, edge - slots), -1.0, F32)
    give_src[0:1] = jnp.concatenate([ids, none], axis=1)
    give_src[8:9] = jnp.concatenate([none, ids], axis=1)
    lane = iota((1, edge), 1)
    owned = jnp.where(lane < slots + MB_DEV, (row * MB_DEV + lane - slots).astype(F32), -2.0)
    asked = jnp.concatenate([jnp.where(used, models_row, -2.0), none], axis=1)
    ask_src[0:1] = jnp.where(lane < slots, asked, owned)
    data_load.wait()
    d = data[...]

    order = far(nz) + [0]
    place = {k: (order.index(k) // 2, order.index(k) % 2) for k in order}
    home = prod.at[place[0][0], 0, place[0][1]]

    high = d.astype(BF16)
    low = (d - high.astype(F32)).astype(BF16)
    u_high, u_low = dot(table_t, high), dot(table_t, low)
    eight = 8
    row_of = lax.rem(iota((2 * eight, edge), 0), eight)
    for k in range(chunks):
        loads[k].wait()
        for pair in range(step // (2 * eight)):
            parts = []
            for half in range(2):
                base = k * step + (2 * pair + half) * eight
                both = jnp.concatenate([u_high[base : base + eight], u_low[base : base + eight]], axis=0)
                left = jnp.concatenate(
                    [jnp.where(row_of == i, both, 0.0).astype(BF16) for i in range(eight)], axis=1
                )
                right = tiles[base : base + eight].reshape(eight * edge, edge)
                out = dot(left, right)
                parts.append(out[:eight] + out[eight:])
            base = k * step + 2 * pair * eight
            home[base : base + 2 * eight] = jnp.concatenate(parts, axis=0).astype(BF16)

    sent = []
    pl.semaphore_wait(barrier, len(greeted))
    for k in far(ny):
        send(ask_src.at[0:1], ask.at[k : k + 1], s_ask, r_ask, peer(dy=k))
    for k in far(nz):
        half = 8 * place[k][1]
        send(give_src.at[half : half + 1], give.at[k : k + 1], s_give, r_give, peer(dz=k))
    for k in far(nz):
        pair, j = place[k]
        send(home, prod.at[pair, 0, j], s_prod.at[pair], r_prod.at[pair], peer(dz=k))
    prods = [
        group(prod.at[pair, 0] if 2 * pair + 2 < nz else prod.at[pair, 0, 0], s_prod.at[pair], r_prod.at[pair])
        for pair in range(nz // 2)
    ]
    asks = group(ask.at[1:ny], s_ask, r_ask)
    gives = group(give.at[1:nz], s_give, r_give)
    relays = [group(prod.at[pair, 1], s_rel, r_rel.at[pair]) for pair in range(nz // 2)]
    relayed = group(prod.at[:, 0], s_rel, r_rel.at[0])

    def relay(k):
        pair, j = place[k]
        send(prod.at[pair, 0, j], prod.at[pair, 1, j], s_rel, r_rel.at[pair], peer(dc=1))

    relay(0)
    sent += [asks, gives, relayed] + prods

    for t in range(slots):
        turned[t] = tiles[t].T
    half = 8 * place[0][1]
    give[0:1] = give_src[half : half + 1]
    gives.wait_recv()
    other_gives = send(give.at[0:nz], give_in, s_give2, r_give2, peer(dc=1))
    sent.append(other_gives)
    per = nz // 4

    def fetch(part):
        for pair in range(part * per, (part + 1) * per):
            prods[pair].wait_recv()
            for k in order[2 * pair : 2 * pair + 2]:
                if k > 0:
                    relay(k)

    asks.wait_recv()
    ask[0:1] = ask_src[0:1]
    ask_cols = ask[...].T
    other_gives.wait_recv()
    for pair in range(nz // 2):
        for i in range(CORES):
            k0, k1 = order[2 * pair], order[2 * pair + 1]
            table = (give, give_in)[i]
            part, lanes = i, pair * edge
            given = jnp.maximum(table[k0 : k0 + 1], table[k1 : k1 + 1])
            for p in range(ny):
                wanted = jnp.broadcast_to(ask_cols[0:wide, p : p + 1], (wide, edge))
                match[part, p * wide : (p + 1) * wide, lanes : lanes + edge] = jnp.where(
                    wanted == given, 1.0, 0.0
                ).astype(BF16)

    def add(part):
        found = dot(match[part], prod[:, part].reshape(nz * slots, edge))
        picked[...] = found if part == 0 else picked[...] + found

    fetch(0)
    fetch(1)
    add(0)
    for pair in range(nz // 2):
        relays[pair].wait_recv()
    add(1)

    sel_src[...] = picked[...].astype(BF16).reshape(ny, wide, edge)
    slot_rows, own_rows = pl.ds(0, slots), pl.ds(slots, wide - slots)
    for k in far(ny):
        send(sel_src.at[k, slot_rows], sel_in.at[k, slot_rows], s_sel, r_sel, peer(dy=-k))
    for k in far(ny):
        send(sel_src.at[k, own_rows], sel_in.at[k, own_rows], s_own, r_own, peer(dy=-k))
    sels = group(sel_in.at[1:ny, slot_rows], s_sel, r_sel)
    owns = group(sel_in.at[1:ny, own_rows], s_own, r_own)
    sent += [sels, owns]
    total = picked[0:slots].astype(BF16).astype(F32)
    sels.wait_recv()
    for k in range(1, ny):
        total = total + sel_in[k, 0:slots].astype(F32)
    v_slots[...] = total

    acc = jnp.zeros((blocks, edge), F32)
    for base in range(0, slots, eight):
        left = []
        for t in range(base, base + eight):
            mine = (first_w <= float(t)) & (last_w > float(t))
            left.append(
                jnp.where(mine, jnp.broadcast_to(v_slots[t : t + 1], (blocks, edge)), 0.0).astype(BF16)
            )
        acc = acc + dot(jnp.concatenate(left, axis=1), turned[base : base + eight].reshape(eight * edge, edge))
    v_own = picked[slots : slots + MB_DEV].astype(BF16).astype(F32)
    owns.wait_recv()
    v_own = v_own + jnp.sum(sel_in[1:ny, slots:wide].astype(F32), axis=0)[0:MB_DEV]

    def over_rows(value):
        return jnp.sum(value, axis=0, keepdims=True)

    x_src[0:blocks] = acc
    terms = [over_rows(v_own * v_own), over_rows(acc * d), over_rows(d * d)]
    x_src[blocks:] = jnp.concatenate(terms + [jnp.zeros((8 - len(terms), edge), F32)], axis=0)
    rows = pl.ds(0, blocks + len(terms))
    for k in far(nx) + [0]:
        for i in range(CORES):
            if k + i > 0:
                send(x_src.at[rows], x_in.at[nx * i + k, rows], s_x, r_x, peer(dx=k, dc=i))
    over_x = group(x_in.at[1 : CORES * nx, rows], s_x, r_x)
    sent.append(over_x)
    over_x.wait_recv()
    own, other = x_src[0 : blocks + 2], x_in[nx, 0 : blocks + 2]
    for k in range(1, nx):
        own = own + x_in[k, 0 : blocks + 2]
        other = other + x_in[nx + k, 0 : blocks + 2]
    g = own[0:blocks]
    g_other = other[0:blocks]
    v_row = own[blocks : blocks + 1] + other[blocks : blocks + 1]
    gd_row = own[blocks + 1 : blocks + 2] + other[blocks + 1 : blocks + 2]
    d_row = x_src[blocks + 2 : blocks + 3] + x_in[nx, blocks + 2 : blocks + 3]
    g_row = over_rows(g * g + g_other * g_other)

    quarter = edge // 4
    stack = jnp.concatenate([g_row, gd_row, d_row, v_row, jnp.zeros((4, edge), F32)], axis=0)
    stack = stack + pltpu.roll(stack, 2 * quarter, 1)
    stack = stack + pltpu.roll(stack, quarter, 1)
    mine = iota((8, edge), 1) // quarter == iota((8, edge), 0)
    f_in[0:1] = over_rows(jnp.where(mine, stack, 0.0))
    for i in far(ny) + [0]:
        for k in far(nz) + [0]:
            slot = i * nz + k
            if slot > 0:
                send(f_in.at[0:1], f_in.at[slot : slot + 1], s_f, r_f, peer(dy=i, dz=k))
    finals = group(f_in.at[1 : ny * nz], s_f, r_f)
    sent.append(finals)
    for stage in sent:
        stage.wait_send()
    finals.wait_recv()
    sums = jnp.broadcast_to(over_rows(f_in[...]), (8, edge))
    sums = jnp.sum(jnp.where(mine, sums, 0.0), axis=1, keepdims=True)
    g_sq, gd, d_sq, v_sq = sums[0:1], sums[1:2], sums[2:3], sums[3:4]
    beta0_sq = d_sq + EPS
    beta0 = jnp.sqrt(beta0_sq)
    alpha_sq = v_sq / beta0_sq + EPS
    alpha = jnp.sqrt(alpha_sq)
    scale = 1.0 / (beta0 * alpha)
    u_sq = g_sq * (scale * scale) - (2.0 / beta0_sq) * gd + (alpha_sq / beta0_sq) * d_sq
    beta_sq = jnp.maximum(u_sq, 0.0) + EPS
    back = 1.0 / jnp.sqrt(beta_sq)
    ray_out[...] = g * (scale * back) - d * (alpha / beta0 * back)
    model_out[...] = v_own * (1.0 / (alpha_sq + beta_sq))


def build(mesh, ny, nz, nx):
    def on_device(tiles, tile_model, ray_counts, data):
        slots, edge = tiles.shape[2], tiles.shape[3]
        blocks = ray_counts.shape[2]
        chunks = 4
        wide = slots + 16
        rows = ny * wide
        integers = jnp.pad(tile_model, ((0, 0), (0, 0), (0, edge - slots))) + jnp.pad(
            ray_counts, ((0, 0), (0, 0), (slots, edge - slots - blocks))
        )
        vmem, dma = pltpu.VMEM, pltpu.SemaphoreType.DMA
        model, rays = pl.pallas_call(
            functools.partial(kernel, ny, nz, nx, slots, blocks, chunks, wide),
            out_shape=(
                jax.ShapeDtypeStruct((MB_DEV, edge), F32),
                jax.ShapeDtypeStruct((blocks, edge), F32),
            ),
            in_specs=[
                pl.BlockSpec(memory_space=pl.ANY),
                pl.BlockSpec(memory_space=pltpu.VMEM),
                pl.BlockSpec(memory_space=pl.ANY),
            ],
            out_specs=(pl.BlockSpec(memory_space=pltpu.VMEM), pl.BlockSpec(memory_space=pltpu.VMEM)),
            scratch_shapes=[
                vmem((slots, edge, edge), BF16),
                vmem((slots, edge, edge), BF16),
                vmem((blocks, edge), F32),
                vmem((16, edge), F32),
                vmem((nz, edge), F32),
                vmem((nz, edge), F32),
                vmem((8, edge), F32),
                vmem((ny, edge), F32),
                vmem((nz // 2, CORES, 2, slots, edge), BF16),
                vmem((2, rows, nz // 2 * CORES * slots), BF16),
                vmem((rows, edge), F32),
                vmem((ny, wide, edge), BF16),
                vmem((ny, wide, edge), BF16),
                vmem((slots, edge), F32),
                vmem((blocks + 8, edge), F32),
                vmem((CORES * nx, blocks + 8, edge), F32),
                vmem((ny * nz, edge), F32),
                dma((chunks,)), dma,
                dma, dma, dma, dma,
                dma, dma,
                dma((nz // 2,)), dma((nz // 2,)),
                dma, dma((nz // 2,)),
                dma, dma,
                dma, dma,
                dma, dma,
                dma, dma,
            ],
            compiler_params=pltpu.CompilerParams(
                collective_id=0, has_side_effects=True, vmem_limit_bytes=55212 * 1024
            ),
        )(tiles, integers, data.reshape(blocks, edge))
        return model.reshape(1, -1), rays.reshape(-1)

    return jax.shard_map(
        on_device,
        mesh=mesh,
        in_specs=(
            P("row", "col", None, None, None),
            P("row", "col", None),
            P("row", "col", None),
            P("row"),
        ),
        out_specs=(P("col", "row"), P("row")),
        check_vma=False,
    )


def solution(mesh):
    nz = 12
    return build(mesh, mesh.shape["row"] // (CORES * nz), nz, mesh.shape["col"])
```
